32 devices in a mesh: dp: 8 (over z, x), mp: 4 (over y, core).
Axes of the slice: x: 2, y: 2, z: 4, core: 2. Of those that a mesh axis runs over, the one named last changes fastest.
Arguments:
- tokens: bfloat16 [32768, 1024], P('dp', 'mp'), may hold values from -6 to 6
- cotangent: bfloat16 [32768, 1024], P('dp', 'mp'), may hold values from -6 to 6
- lengths: int32 [32], P('dp'), may hold values from 128 to 1024, as said below
- norm_gain: float32 [2, 1024], replicated, may hold values from 0.5 to 1.5
- norm_shift: float32 [2, 1024], replicated, may hold values from -3 to 3
- qkv_weight: bfloat16 [1024, 3072], P(None, 'mp'), may hold values from -0.1875 to 0.1875
- out_weight: bfloat16 [1024, 1024], P('mp'), may hold values from -0.75 to 0.75
- up_weight: bfloat16 [1024, 4096], P(None, 'mp'), may hold values from -0.1875 to 0.1875
- down_weight: bfloat16 [4096, 1024], P('mp'), may hold values from -0.09375 to 0.09375
- qkv_bias: float32 [3072], P('mp'), may hold values from -3 to 3
- up_bias: float32 [4096], P('mp'), may hold values from -3 to 3
- res_bias: float32 [2, 1024], P(None, 'mp'), may hold values from -3 to 3
- in_factor: float32 [2, 1024, 128], P(None, ('dp', 'mp')), may hold values from -0.1875 to 0.1875
- qkv_factor: float32 [128, 3072], P('dp', 'mp'), may hold values from -0.5 to 0.5
- up_factor: float32 [128, 4096], P('dp', 'mp'), may hold values from -0.5 to 0.5
- out_factor: float32 [1024, 128], P('mp', 'dp'), may hold values from -0.75 to 0.75
- down_factor: float32 [4096, 128], P('mp', 'dp'), may hold values from -0.09375 to 0.09375
- res_factor: float32 [2, 128, 1024], P(None, 'dp', 'mp'), may hold values from -0.5 to 0.5
- in_moments: float32 [2, 2, 1024, 128], P(None, None, ('dp', 'mp')), may hold values from -6 to 6, as said below
- qkv_moments: float32 [2, 128, 3072], P(None, 'dp', 'mp'), may hold values from -6 to 6, as said below
- up_moments: float32 [2, 128, 4096], P(None, 'dp', 'mp'), may hold values from -6 to 6, as said below
- out_moments: float32 [2, 1024, 128], P(None, 'mp', 'dp'), may hold values from -6 to 6, as said below
- down_moments: float32 [2, 4096, 128], P(None, 'mp', 'dp'), may hold values from -6 to 6, as said below
- res_moments: float32 [2, 2, 128, 1024], P(None, None, 'dp', 'mp'), may hold values from -6 to 6, as said below
Outputs:
- result: float32 [32768, 1024], P('dp', 'mp')
- grad_tokens: float32 [32768, 1024], P('dp', 'mp')
- in_grad: float32 [2, 1024, 128], P(None, ('dp', 'mp'))
- qkv_grad: float32 [128, 3072], P('dp', 'mp')
- up_grad: float32 [128, 4096], P('dp', 'mp')
- out_grad: float32 [1024, 128], P('mp', 'dp')
- down_grad: float32 [4096, 128], P('mp', 'dp')
- res_grad: float32 [2, 128, 1024], P(None, 'dp', 'mp')
- merged_qkv: float32 [1024, 3072], P(None, 'mp')
- merged_out: float32 [1024, 1024], P('mp')
- merged_up: float32 [1024, 4096], P(None, 'mp')
- merged_down: float32 [4096, 1024], P('mp')
- in_pruned: float32 [2, 2, 1024, 128], P(None, None, ('dp', 'mp'))
- qkv_pruned: float32 [2, 128, 3072], P(None, 'dp', 'mp')
- up_pruned: float32 [2, 128, 4096], P(None, 'dp', 'mp')
- out_pruned: float32 [2, 1024, 128], P(None, 'mp', 'dp')
- down_pruned: float32 [2, 4096, 128], P(None, 'mp', 'dp')
- res_pruned: float32 [2, 2, 128, 1024], P(None, None, 'dp', 'mp')
The draws below stay inside these ranges and needn't reach their ends.
Inputs may be any that keep to these rules, and one draw needn't show every extreme that they name: `lengths`: one sequence, chosen by the seed, has exactly 1024. `in_moments`: first member normal, second member between 0.5 and 5. `qkv_moments`: first member normal, second member between 0.5 and 5. `up_moments`: first member normal, second member between 0.5 and 5. `out_moments`: first member normal, second member between 0.5 and 5. `down_moments`: first member normal, second member between 0.5 and 5. `res_moments`: first member normal, second member between 0.5 and 5.
All inputs are finite; a program needn't handle non-finite values.
Results may differ from the reference program's by a relative error of at most 0.0095.
The reference program's roundings to bfloat16 on the way count: a program that leaves them out, or rounds other values in their place, can miss the bound.
Values may be sent and summed in bfloat16 or wider, within the bound.
No kernel may reach another device: no remote copies, remote signals or barrier semaphores. Data moves between devices by JAX's collectives and lax.ppermute only.
A program may use at most 256 MiB of HBM per device.

```python
import math
import jax
import jax.numpy as jnp
from jax import lax

D = 1024
HEADS = 16
HEAD = 64
ROT = 16
FF = 4096
RANK = 128
LEN = 1024
SEQS = 32
TOKENS = 32768


def draw_lengths(key, part):
    key = jax.random.fold_in(key, 1)
    first_key, second_key = jax.random.split(key)
    drawn = jax.random.randint(first_key, (SEQS,), LEN // 8, LEN + 1)
    chosen = jax.random.randint(second_key, (), 0, SEQS)
    return jnp.where(jnp.arange(SEQS) == chosen, LEN, drawn).astype(jnp.int32)


def moment_pair(key, shape):
    first_key, second_key = jax.random.split(key)
    first_moment = jnp.clip(jax.random.normal(first_key, shape, jnp.float32), -6.0, 6.0)
    second_moment = jnp.exp(jax.random.uniform(second_key, shape, jnp.float32, math.log(0.5), math.log(5.0)))
    return jnp.stack([first_moment, second_moment])


def draw_in_moments(key, part):
    key = jax.random.fold_in(key, 2)
    return moment_pair(key, (2, D, RANK))


def draw_qkv_moments(key, part):
    key = jax.random.fold_in(key, 3)
    return moment_pair(key, (RANK, 3 * D))


def draw_up_moments(key, part):
    key = jax.random.fold_in(key, 4)
    return moment_pair(key, (RANK, FF))


def draw_out_moments(key, part):
    key = jax.random.fold_in(key, 5)
    return moment_pair(key, (D, RANK))


def draw_down_moments(key, part):
    key = jax.random.fold_in(key, 6)
    return moment_pair(key, (FF, RANK))


def draw_res_moments(key, part):
    key = jax.random.fold_in(key, 7)
    return moment_pair(key, (2, RANK, D))


def block_scale(stream_key, shape, cuts, low, largest):
    level = 1.0
    for dim, blocks in cuts:
        steps = jax.random.uniform(jax.random.fold_in(jax.random.fold_in(stream_key, 6), dim), (blocks,), jnp.float32, low / len(cuts), largest / len(cuts))
        level = level * jnp.repeat(jnp.exp(steps), shape[dim] // blocks).reshape((-1,) + (1,) * (len(shape) - 1 - dim))
    return level


def gaussian(rng, shape, scale, reach, cuts=(), held_as=jnp.bfloat16):
    values = scale * jax.random.normal(rng, shape, jnp.float32)
    if cuts:
        values = values * block_scale(rng, shape, cuts, -0.22, 0.18)
    return jnp.clip(values, -reach, reach).astype(held_as)


def setup_inputs(seed: int = 0) -> dict:
    streams_of = jax.random.split(jax.random.key(seed), 25)
    return {
        "tokens": gaussian(streams_of[0], (TOKENS, D), 1.0, 6.0, ((0, 8), (1, 4))),
        "cotangent": gaussian(streams_of[1], (TOKENS, D), 1.0, 6.0, ((0, 8), (1, 4))),
        "lengths": draw_lengths(jax.random.fold_in(streams_of[24], 71), 0),
        "norm_gain": jnp.clip(1.0 + 0.1 * jax.random.normal(streams_of[3], (2, D), jnp.float32), 0.5, 1.5),
        "norm_shift": gaussian(streams_of[4], (2, D), 0.5, 3.0, (), jnp.float32),
        "qkv_weight": gaussian(streams_of[5], (D, 3 * D), D ** -0.5, 0.1875, ((1, 4),)),
        "out_weight": gaussian(streams_of[6], (D, D), (D // 16) ** -0.5, 0.75, ((0, 4),)),
        "up_weight": gaussian(streams_of[7], (D, FF), D ** -0.5, 0.1875, ((1, 4),)),
        "down_weight": gaussian(streams_of[8], (FF, D), FF ** -0.5, 0.09375, ((0, 4),)),
        "qkv_bias": gaussian(streams_of[9], (3 * D,), 0.5, 3.0, ((0, 4),), jnp.float32),
        "up_bias": gaussian(streams_of[10], (FF,), 0.5, 3.0, ((0, 4),), jnp.float32),
        "res_bias": gaussian(streams_of[11], (2, D), 0.5, 3.0, ((1, 4),), jnp.float32),
        "in_factor": gaussian(streams_of[12], (2, D, RANK), D ** -0.5, 0.1875, ((1, 32),), jnp.float32),
        "qkv_factor": gaussian(streams_of[13], (RANK, 3 * D), RANK ** -0.5, 0.5, ((0, 8), (1, 4)), jnp.float32),
        "up_factor": gaussian(streams_of[14], (RANK, FF), RANK ** -0.5, 0.5, ((0, 8), (1, 4)), jnp.float32),
        "out_factor": gaussian(streams_of[15], (D, RANK), (D // 16) ** -0.5, 0.75, ((0, 4), (1, 8)), jnp.float32),
        "down_factor": gaussian(streams_of[16], (FF, RANK), FF ** -0.5, 0.09375, ((0, 4), (1, 8)), jnp.float32),
        "res_factor": gaussian(streams_of[17], (2, RANK, D), RANK ** -0.5, 0.5, ((1, 8), (2, 4)), jnp.float32),
        "in_moments": draw_in_moments(jax.random.fold_in(streams_of[24], 71), 0),
        "qkv_moments": draw_qkv_moments(jax.random.fold_in(streams_of[24], 71), 0),
        "up_moments": draw_up_moments(jax.random.fold_in(streams_of[24], 71), 0),
        "out_moments": draw_out_moments(jax.random.fold_in(streams_of[24], 71), 0),
        "down_moments": draw_down_moments(jax.random.fold_in(streams_of[24], 71), 0),
        "res_moments": draw_res_moments(jax.random.fold_in(streams_of[24], 71), 0),
    }


@jax.custom_vjp
def low(v):
    return lax.optimization_barrier(v.astype(jnp.bfloat16)).astype(jnp.float32)

@jax.custom_vjp
def low_back(v):
    return v

def low_keep(v):
    return (low(v), None)

def low_pass(kept, grad):
    return (grad,)

def back_keep(v):
    return (v, None)

def back_low(kept, grad):
    return (low(grad),)
low.defvjp(low_keep, low_pass)
low_back.defvjp(back_keep, back_low)
first_fix = 1.0 - math.exp(100.0 * math.log(0.9))
second_fix = 1.0 - math.exp(100.0 * math.log(0.999))

def exact_product(left_side, right_side):
    return jnp.dot(left_side, right_side, precision=lax.Precision.HIGHEST, preferred_element_type=jnp.float32)

def normalize(values, gain_row, shift_row):
    centred = values - lax.optimization_barrier(jnp.mean(values, -1, keepdims=True))
    norm_scale = lax.rsqrt(lax.optimization_barrier(jnp.mean(centred * centred, -1, keepdims=True)) + 1e-05)
    return centred * norm_scale * gain_row + shift_row

def rotary_tables(length):
    half_rot = ROT // 2
    frequency = 10000.0 ** (-jnp.arange(half_rot, dtype=jnp.float32) * 2.0 / ROT)
    angles = jnp.arange(length, dtype=jnp.float32)[:, None] * frequency[None, :]
    return (jnp.cos(angles)[:, None, :], jnp.sin(angles)[:, None, :])

def rotate(values, cosine_table, sine_table):
    half_rot = ROT // 2
    first_part = values[..., :half_rot]
    second_part = values[..., half_rot:ROT]
    return jnp.concatenate([first_part * cosine_table - second_part * sine_table, second_part * cosine_table + first_part * sine_table, values[..., ROT:]], -1)

def sequence_forward(inputs, seq_length, frozen, factors, norm_gain, norm_shift, qkv_bias, up_bias, res_bias):
    qkv_weight, out_weight, up_weight, down_weight = frozen
    in_factor, qkv_factor, up_factor, out_factor, down_factor, res_factor = factors
    first_low = low(normalize(inputs, norm_gain[0], norm_shift[0]))
    second_low = low(normalize(inputs, norm_gain[1], norm_shift[1]))
    qkv_rank = low(exact_product(first_low, in_factor[0]))
    mixed_rows = low_back(exact_product(first_low, qkv_weight) + exact_product(qkv_rank, qkv_factor) + qkv_bias)
    mixed_rows = mixed_rows.reshape(LEN, HEADS, 3, HEAD)
    cosine_table, sine_table = rotary_tables(LEN)
    queries = low(rotate(mixed_rows[:, :, 0], cosine_table, sine_table))
    key_side = low(rotate(mixed_rows[:, :, 1], cosine_table, sine_table))
    values = low(mixed_rows[:, :, 2])
    scores = low_back(jnp.einsum('qhd,khd->hqk', queries, key_side, precision=lax.Precision.HIGHEST) * HEAD ** (-0.5))
    position = jnp.arange(LEN)
    allowed = (position[None, :] <= position[:, None]) & (position[None, :] < seq_length)
    scores = jnp.where(allowed[None], scores, -1e+30)
    highest = lax.optimization_barrier(jnp.max(scores, -1, keepdims=True))
    weights = jnp.exp(scores - highest)
    probabilities = weights / lax.optimization_barrier(jnp.sum(weights, -1, keepdims=True))
    context = low(low_back(jnp.einsum('hqk,khd->qhd', low(probabilities), values, precision=lax.Precision.HIGHEST))).reshape(LEN, D)
    out_rank = low(low_back(exact_product(context, out_factor)))
    up_rank = low(exact_product(second_low, in_factor[1]))
    hidden = low_back(exact_product(second_low, up_weight) + exact_product(up_rank, up_factor) + up_bias)
    active = low(jax.nn.gelu(hidden, approximate=False))
    down_rank = low(low_back(exact_product(active, down_factor)))
    result = inputs + exact_product(context, out_weight) + exact_product(active, down_weight) + exact_product(out_rank, res_factor[0]) + exact_product(down_rank, res_factor[1]) + res_bias[0] + res_bias[1]
    return jnp.where((position < seq_length)[:, None], result, 0.0)

def adam_step(factor, moment, gradient):
    first_moment = 0.9 * moment[0] + 0.1 * gradient
    second_moment = 0.999 * moment[1] + 0.001 * gradient * gradient
    updated = factor - 0.01 * (first_moment / first_fix) / (jnp.sqrt(second_moment / second_fix) + 1e-08)
    keep_mask = (jnp.abs(moment[0]) >= 0.5).astype(jnp.float32)
    return (updated, jnp.stack([first_moment * keep_mask, second_moment * keep_mask]))

def reference(tokens, cotangent, lengths, norm_gain, norm_shift, qkv_weight, out_weight, up_weight, down_weight, qkv_bias, up_bias, res_bias, in_factor, qkv_factor, up_factor, out_factor, down_factor, res_factor, in_moments, qkv_moments, up_moments, out_moments, down_moments, res_moments):
    frozen = (qkv_weight.astype(jnp.float32), out_weight.astype(jnp.float32), up_weight.astype(jnp.float32), down_weight.astype(jnp.float32))

    def block_forward(inputs, in_f, qkv_f, up_f, out_f, down_f, res_f):
        factors = (low(in_f), low(qkv_f), low(up_f), low(out_f), low(down_f), low(res_f))

        def one_sequence(pieces):
            return sequence_forward(pieces[0], pieces[1], frozen, factors, norm_gain, norm_shift, qkv_bias, up_bias, res_bias)
        outputs = lax.map(jax.checkpoint(one_sequence), (inputs.reshape(SEQS, LEN, D), lengths))
        return outputs.reshape(SEQS * LEN, D)
    result, pullback = jax.vjp(block_forward, tokens.astype(jnp.float32), in_factor, qkv_factor, up_factor, out_factor, down_factor, res_factor)
    gradients = pullback(cotangent.astype(jnp.float32))
    new_in, in_pruned = adam_step(in_factor, in_moments, gradients[1])
    new_qkv, qkv_pruned = adam_step(qkv_factor, qkv_moments, gradients[2])
    new_up, up_pruned = adam_step(up_factor, up_moments, gradients[3])
    new_out, out_pruned = adam_step(out_factor, out_moments, gradients[4])
    new_down, down_pruned = adam_step(down_factor, down_moments, gradients[5])
    new_res, res_pruned = adam_step(res_factor, res_moments, gradients[6])
    merged_qkv = frozen[0] + exact_product(new_in[0], new_qkv)
    merged_out = frozen[1] + exact_product(new_out, new_res[0])
    merged_up = frozen[2] + exact_product(new_in[1], new_up)
    merged_down = frozen[3] + exact_product(new_down, new_res[1])
    return (result, gradients[0], gradients[1], gradients[2], gradients[3], gradients[4], gradients[5], gradients[6], merged_qkv, merged_out, merged_up, merged_down, in_pruned, qkv_pruned, up_pruned, out_pruned, down_pruned, res_pruned)
```

```python
import functools
import math

import jax
import jax.numpy as jnp
from jax import lax
from jax.experimental import pallas as pl
from jax.experimental.pallas import tpu as pltpu
from jax.sharding import PartitionSpec as P

HEAD = 64
ROT = 16
BF = jnp.bfloat16
F32 = jnp.float32

first_fix = 1.0 - math.exp(100.0 * math.log(0.9))
second_fix = 1.0 - math.exp(100.0 * math.log(0.999))


def mm(a, b):
    return lax.dot_general(a, b, (((1,), (0,)), ((), ())), preferred_element_type=F32)


def mm_t(a, b):
    return lax.dot_general(a, b, (((1,), (1,)), ((), ())), preferred_element_type=F32)


def rows_mm(a, b):
    return lax.dot_general(a, b, (((0,), (0,)), ((), ())), preferred_element_type=F32)


def layer_norm(x):
    centred = x - jnp.mean(x, -1, keepdims=True)
    scale = lax.rsqrt(jnp.mean(centred * centred, -1, keepdims=True) + 1e-05)
    return centred * scale, scale


def layer_norm_back(grad_unit, unit_rows, scale):
    return scale * (
        grad_unit
        - jnp.mean(grad_unit, -1, keepdims=True)
        - unit_rows * jnp.mean(grad_unit * unit_rows, -1, keepdims=True)
    )


def rotate(values, cos, sin_a, sin_b, sign):
    width = values.shape[-1]
    turned = pltpu.roll(values, width - ROT // 2, 1) * sin_a + pltpu.roll(values, ROT // 2, 1) * sin_b
    return values * cos + turned if sign > 0 else values * cos - turned


def input_pairs(sizes, core, sources, fin_v, res_places):
    high, folds, ranks, rank, own_cols, direct = sizes
    if not direct:
        f_in, f_res = sources
        return [(f_in, fin_v), (f_res.at[0], res_places[0]), (f_res.at[1], res_places[1])]
    width = 2 * folds * rank + 2 * own_cols
    found = []
    for c in range(2):
        deep, wide2 = sources[c], sources[2 + c]
        which = core if c == 0 else 1 - core
        for y in range(high):
            for n in range(2):
                for j in range(folds):
                    at = y * width + (n * folds + j) * rank
                    rows = pl.ds(pl.multiple_of(((y * 2 + which) * folds + j) * ranks, ranks), ranks)
                    found.append((deep.at[:, :, at : at + rank], fin_v.at[n, :, rows, :]))
                at = y * width + 2 * folds * rank + n * own_cols
                place = pl.ds(pl.multiple_of((y * 2 + which) * own_cols, own_cols), own_cols)
                found.append((wide2.at[:, at : at + own_cols], res_places[n].at[:, place]))
    return found


def block_kernel(cfg, scal, *refs):
    chunk, seqs, first, last, length, tile, parts, cols, dim, wide, units, rank, sizes, n_src = cfg
    whole_rows, refs = refs[:4], refs[4:]
    received, refs = refs[: 2 * parts - 4], refs[2 * parts - 4 :]
    (gain, shift, b_qkv, b_up, rope, w_qkv, w_up, w_down, w_out, f_split), refs = refs[:10], refs[10:]
    sources, refs = refs[:n_src], refs[n_src:]
    (acc_in, res_in, keep, send), refs = refs[:4], refs[4:]
    sums, refs = refs[: len(refs) - 31], refs[len(refs) - 31 :]
    (
        fin_v, gin_b, gres_b, gsplit_b, x_v, c_v, wq_v, wu_v, wd_v, ft_v, rope_v, acc_v, res_v,
        q_s, k_s, v_s, g_s, qt_s, gt_s, gq_s, gkt_s, gvt_s, ac_s, p_s, qr_s, gor_s, out_v,
        row_sems, w_sems, out_sems, acc_sems,
    ) = refs
    me = scal[seqs]
    core = lax.rem(me, 2)
    steps = length // tile
    mixed_cols = 3 * wide
    joint = units + wide

    def tiles_of(s):
        return (scal[s] + tile - 1) // tile

    def row_slice(t, size=tile):
        return pl.ds(pl.multiple_of(t * tile, tile), size)


    def row_copies(s, t):
        found = []
        slot = lax.rem(s, 2)
        for which, dest in enumerate((x_v, c_v)):
            for k in range(parts):
                at = pl.ds(pl.multiple_of(s * length + t * tile, tile), tile)
                if k < 2:
                    src = whole_rows[2 * k + which].at[
                        pl.ds(pl.multiple_of((chunk * seqs + s) * length + t * tile, tile), tile), :
                    ]
                else:
                    src = received[2 * (k - 2) + which].at[at, :]
                place = pl.ds(pl.multiple_of(jnp.bitwise_xor(me, k) * cols, cols), cols)
                found.append(
                    pltpu.make_async_copy(
                        src, dest.at[slot, row_slice(t), place], row_sems.at[slot, t, which * parts + k]
                    )
                )
        return found

    def start_rows(s):
        def one(t, carry):
            for copy in row_copies(s, t):
                copy.start()
            return carry

        lax.fori_loop(0, tiles_of(s), one, 0)

    def out_copies(s, t):
        found = []
        for which in range(2):
            for k in range(parts):
                place = pl.ds(pl.multiple_of(jnp.bitwise_xor(me, k) * cols, cols), cols)
                target = keep if k % 2 == 0 else send
                at = (k // 2) * cols
                rows = pl.ds(pl.multiple_of(s * length + t * tile, tile), tile)
                found.append(
                    pltpu.make_async_copy(
                        out_v.at[which, row_slice(t), place],
                        target.at[which, rows, at : at + cols],
                        out_sems.at[t, which * parts + k],
                    )
                )
        return found

    def drain(s):
        def one(t, carry):
            for copy in out_copies(s, t):
                copy.wait()
            return carry

        lax.fori_loop(0, tiles_of(s), one, 0)

    res_places = (wd_v.at[joint + rank :, :dim], wd_v.at[joint : joint + rank, :dim])
    pairs = [
        (w_qkv, wq_v.at[:dim, :mixed_cols]),
        (f_split.at[:, :mixed_cols], wq_v.at[dim:, :mixed_cols]),
        (rope, rope_v),
        (w_up, wu_v.at[:dim, :units]),
        (f_split.at[:, mixed_cols : mixed_cols + units], wu_v.at[dim:, :units]),
        (w_down, wd_v.at[:units, :dim]),
        (w_out, wd_v.at[units:joint, :dim]),
        (f_split.at[:, mixed_cols + units :], ft_v),
    ] + input_pairs(sizes, core, sources, fin_v, res_places)
    loads = [pltpu.make_async_copy(a, b, w_sems.at[i]) for i, (a, b) in enumerate(pairs)]
    start_rows(0)
    for load in loads:
        load.start()
    back_in = []
    if first:
        acc_v[...] = jnp.zeros_like(acc_v)
        res_v[...] = jnp.zeros_like(res_v)
    else:
        back_in = [
            pltpu.make_async_copy(acc_in, acc_v, acc_sems.at[0]),
            pltpu.make_async_copy(res_in, res_v, acc_sems.at[1]),
        ]
        for copy in back_in:
            copy.start()
    wd_v[:units, dim + rank :] = jnp.zeros((units, rank), BF)
    wd_v[units:joint, dim : dim + rank] = jnp.zeros((wide, rank), BF)
    for load in loads:
        load.wait()
    for copy in back_in:
        copy.wait()
    wd_v[:units, dim : dim + rank] = ft_v[:, :units].astype(F32).T.astype(BF)
    wd_v[units:joint, dim + rank :] = ft_v[:, units:].astype(F32).T.astype(BF)
    wq_v[:dim, mixed_cols:] = fin_v[0].reshape(dim, rank)
    wu_v[:dim, units:] = fin_v[1].reshape(dim, rank)

    def whole(ref, top, depth, width, cut, other, at):
        def one(i, carry):
            rows = pl.ds(pl.multiple_of(top + i * cut, cut), cut)
            low_rank = mm(ref[rows, at : at + rank], other())
            ref[rows, :width] = (ref[rows, :width].astype(F32) + low_rank).astype(BF)
            return carry

        lax.fori_loop(0, depth // cut, one, 0)

    cut = min(256, units, wide)
    whole(wu_v, 0, dim, units, cut, lambda: wu_v[dim:, :units], units)
    whole(wd_v, 0, units, dim, cut, lambda: wd_v[joint : joint + rank, :dim], dim)
    whole(wd_v, units, wide, dim, cut, lambda: wd_v[joint + rank :, :dim], dim + rank)

    c_in0, c_in1, c_qkv, c_up, c_down, c_out = (
        slice(0, dim),
        slice(dim, 2 * dim),
        slice(2 * dim, 2 * dim + mixed_cols),
        slice(2 * dim + mixed_cols, 2 * dim + mixed_cols + units),
        slice(2 * dim + mixed_cols + units, 2 * dim + mixed_cols + 2 * units),
        slice(2 * dim + mixed_cols + 2 * units, 2 * dim + mixed_cols + 2 * units + wide),
    )
    lane = lax.broadcasted_iota(jnp.int32, (1, 128), 1)
    left = lane < HEAD

    def one_sequence(s, carry):
        seq_len = scal[s]
        count = tiles_of(s)
        slot = lax.rem(s, 2)

        @pl.when(s + 1 < seqs)
        def _():
            start_rows(s + 1)

        gkt_s[...] = jnp.zeros_like(gkt_s)
        gvt_s[...] = jnp.zeros_like(gvt_s)

        def upstream(t, size):
            position = t * tile + lax.broadcasted_iota(jnp.int32, (size, 1), 0)
            return jnp.where(position < seq_len, c_v[slot, row_slice(t, size), :].astype(F32), 0.0).astype(BF)

        def tables(t, size):
            rows = row_slice(t, size)
            return [jnp.concatenate([rope_v[i, rows, :]] * (wide // 128), 1) for i in range(3)]

        def forward(t, size):
            rows = row_slice(t, size)
            for j in range(size // tile):
                for copy in row_copies(s, t + j):
                    copy.wait()
            unit, _ = layer_norm(x_v[slot, rows, :].astype(F32))
            low_one = (unit * gain[0:1, :] + shift[0:1, :]).astype(BF)
            low_two = (unit * gain[1:2, :] + shift[1:2, :]).astype(BF)
            ups = upstream(t, size)
            hidden = mm(low_two, wu_v[:dim, :])
            back = mm_t(ups, wd_v[:, :dim])
            mixed = mm(low_one, wq_v[:dim, :])
            code_up = hidden[:, units:]
            hidden = hidden[:, :units] + b_up[...]
            code_qkv = mixed[:, mixed_cols:]
            mixed = mixed[:, :mixed_cols] + mm(code_qkv.astype(BF), wq_v[dim:, :mixed_cols]) + b_qkv[...]
            blocks = [mixed[:, i * 128 : (i + 1) * 128] for i in range(mixed_cols // 128)]
            cat = lambda found: jnp.concatenate(found, 1) if len(found) > 1 else found[0]
            q_mixed = cat([jnp.where(left, blocks[3 * p], blocks[3 * p + 1]) for p in range(wide // 128)])
            k_mixed = cat(
                [pltpu.roll(jnp.where(left, blocks[3 * p + 2], blocks[3 * p]), HEAD, 1) for p in range(wide // 128)]
            )
            v_mixed = cat([jnp.where(left, blocks[3 * p + 1], blocks[3 * p + 2]) for p in range(wide // 128)])
            cdf = 0.5 * (1.0 + lax.erf(hidden * (1.0 / math.sqrt(2.0))))
            active = (hidden * cdf).astype(BF)
            slope = cdf + hidden * (jnp.exp(-0.5 * hidden * hidden) * (1.0 / math.sqrt(2.0 * math.pi)))
            grad_hidden = (back[:, :units] * slope).astype(BF)
            ac_s[rows, :units] = active
            cos, sin_a, sin_b = tables(t, size)
            query = rotate(q_mixed, cos, sin_a, sin_b, 1).astype(BF).astype(F32) * HEAD**-0.5
            q_s[rows, :] = query.astype(BF)
            qt_s[:, rows] = query.T.astype(BF)
            k_s[rows, :] = rotate(k_mixed, cos, sin_a, sin_b, 1).astype(BF)
            v_s[rows, :] = v_mixed.astype(BF)
            qr_s[:, rows] = code_qkv.T.astype(BF)
            grad_context = back[:, units:joint]
            g_s[rows, :] = grad_context.astype(BF)
            gt_s[:, rows] = grad_context.T.astype(BF)
            gor_s[:, rows] = back[:, joint + rank :].T.astype(BF)
            below = mm_t(grad_hidden, wu_v[:, :units])
            p_s[rows, :] = below[:, :dim] * gain[1:2, :]
            acc_v[:, c_up] += mm(code_up.T.astype(BF), grad_hidden)
            acc_v[:, c_down] += mm(back[:, joint : joint + rank].T.astype(BF), active)
            acc_v[:, c_in1] += mm(below[:, dim:].T.astype(BF), low_two)

        def finish(t, size):
            rows = row_slice(t, size)
            cos, sin_a, sin_b = tables(t, size)
            grad_q = rotate(gq_s[rows, :], cos, sin_a, sin_b, -1)
            grad_k = rotate(gkt_s[:, rows].T, cos, sin_a, sin_b, -1)
            grad_v = gvt_s[:, rows].T
            blocks = []
            for p in range(wide // 128):
                pair = slice(p * 128, (p + 1) * 128)
                one_q, one_k, one_v = grad_q[:, pair], pltpu.roll(grad_k[:, pair], HEAD, 1), grad_v[:, pair]
                blocks += [jnp.where(left, one_q, one_k), jnp.where(left, one_v, one_q), jnp.where(left, one_k, one_v)]
            grad_mixed = jnp.concatenate(blocks, 1).astype(BF)
            below = mm_t(grad_mixed, wq_v[:, :mixed_cols])
            both = ac_s[rows, :]
            ahead = mm(both, wd_v[:joint, :])
            unit, scale = layer_norm(x_v[slot, rows, :].astype(F32))
            low_one = (unit * gain[0:1, :] + shift[0:1, :]).astype(BF)
            out_v[0, rows, :] = ahead[:, :dim].astype(BF)
            grad_code = below[:, dim:]
            grad_norm = below[:, :dim] + mm_t(grad_code.astype(BF), wq_v[:dim, mixed_cols:])
            grad_unit = grad_norm * gain[0:1, :] + p_s[rows, :]
            out_v[1, rows, :] = layer_norm_back(grad_unit, unit, scale).astype(BF)
            for j in range(size // tile):
                for copy in out_copies(s, t + j):
                    copy.start()
            acc_v[:, c_in0] += mm(grad_code.T.astype(BF), low_one)
            acc_v[:, c_qkv] += mm(qr_s[:, rows], grad_mixed)
            acc_v[:, c_out] += mm(gor_s[:, rows], both[:, units:])
            res_v[...] += mm(ahead[:, dim:].T.astype(BF), upstream(t, size))

        def over_rows(work):
            def single(j, carry):
                work(j, tile)
                return carry

            lax.fori_loop(0, count, single, 0)

        over_rows(forward)

        for i in range(steps):
            @pl.when(i < count)
            def _(i=i):
                qrows = pl.ds(i * tile, tile)
                before, extent = i * tile, (i + 1) * tile
                qpos = before + lax.broadcasted_iota(jnp.int32, (tile, tile), 0)
                kpos = before + lax.broadcasted_iota(jnp.int32, (tile, tile), 1)
                allowed = (kpos <= qpos) & (kpos < seq_len)
                allowed = jnp.concatenate([allowed, allowed], 0)
                def one_pair(p, carry):
                    pair = pl.ds(pl.multiple_of(p * 128, 128), 128)
                    q_all, g_all = q_s[qrows, pair], g_s[qrows, pair]
                    zero = jnp.zeros_like(q_all)
                    q_two = jnp.concatenate([jnp.where(left, q_all, zero), jnp.where(left, zero, q_all)], 0)
                    g_two = jnp.concatenate([jnp.where(left, g_all, zero), jnp.where(left, zero, g_all)], 0)
                    keys, vals = k_s[:extent, pair], v_s[:extent, pair]
                    scores = mm_t(q_two, keys)
                    grad_probs = mm_t(g_two, vals)
                    last = jnp.where(allowed, scores[:, before:], -1e30)
                    scores = jnp.concatenate([scores[:, :before], last], 1) if i else last
                    weights = jnp.exp(scores - jnp.max(scores, -1, keepdims=True))
                    probs = weights * (1.0 / jnp.sum(weights, -1, keepdims=True))
                    low_probs = probs.astype(BF)
                    context = mm(low_probs, vals)
                    row_term = jnp.sum(probs * grad_probs, -1, keepdims=True)
                    grad_scores = (probs * (grad_probs - row_term)).astype(BF)
                    grad_q = mm(grad_scores, keys)
                    ac_s[qrows, pl.ds(pl.multiple_of(units + p * 128, 128), 128)] = jnp.where(
                        left, context[:tile], context[tile:]
                    ).astype(BF)
                    gq_s[qrows, pair] = jnp.where(left, grad_q[:tile], grad_q[tile:]) * HEAD**-0.5
                    for h in range(2):
                        feats = pl.ds(pl.multiple_of(p * 128 + h * HEAD, HEAD), HEAD)
                        part = slice(h * tile, (h + 1) * tile)
                        gkt_s[feats, :extent] += mm(qt_s[feats, qrows], grad_scores[part])
                        gvt_s[feats, :extent] += mm(gt_s[feats, qrows], low_probs[part])
                    return carry

                lax.fori_loop(0, wide // 128, one_pair, 0)

        @pl.when(s > 0)
        def _():
            drain(s - 1)

        over_rows(finish)
        return carry

    lax.fori_loop(0, seqs, one_sequence, 0)
    if not last:
        targets = [(acc_v, sums[0]), (res_v, sums[1])]
    else:
        high, folds, ranks, _, own_cols, direct = sizes
        gsplit_b[...] = acc_v[:, 2 * dim :].astype(BF)
        gres_b[:rank, :] = res_v[rank:, :].astype(BF)
        gres_b[rank:, :] = res_v[:rank, :].astype(BF)
        for n, place in enumerate((c_in0, c_in1)):
            gin_b[n] = acc_v[:, place].T.astype(BF).reshape(gin_b.shape[1:])
        targets = [(gsplit_b, sums[0])]
        if not direct:
            targets += [(gin_b, sums[1]), (gres_b, sums[2])]
        else:
            for c in range(2):
                which = core if c == 0 else 1 - core
                for y in range(high):
                    for n in range(2):
                        for j in range(folds):
                            at = (n * folds + j) * rank
                            rows = pl.ds(pl.multiple_of(((y * 2 + which) * folds + j) * ranks, ranks), ranks)
                            targets.append((gin_b.at[n, :, rows, :], sums[1 + c].at[y, :, :, at : at + rank]))
                        place = pl.ds(pl.multiple_of((y * 2 + which) * own_cols, own_cols), own_cols)
                        targets.append(
                            (gres_b.at[n * rank : (n + 1) * rank, place],
                             sums[3 + c].at[y, :, n * own_cols : (n + 1) * own_cols])
                        )
    back_out = [pltpu.make_async_copy(a, b, acc_sems.at[2 + i]) for i, (a, b) in enumerate(targets)]
    for copy in back_out:
        copy.start()
    drain(seqs - 1)
    for copy in back_out:
        copy.wait()


def block_call(chunk, seqs, last, sizes, acc, scal, whole_rows, received, small, weights, factors, length, parts):
    gain, shift, b_qkv, b_up, rope = small
    w_qkv, w_up, w_down, w_out = weights
    f_split, sources = factors
    dim, units, wide, rank = w_up.shape[0], w_up.shape[1], w_out.shape[0], f_split.shape[0]
    high, folds, ranks, _, own_cols, direct = sizes
    dp = rank // ranks
    cols = dim // parts
    tile = 256 if length % 256 == 0 else 128
    steps = length // tile
    first = acc is None
    acc_shape = jax.ShapeDtypeStruct((rank, 2 * dim + 4 * wide + 2 * units), F32)
    res_shape = jax.ShapeDtypeStruct((2 * rank, dim), F32)
    if first:
        acc = (jnp.zeros((8, 128), F32), jnp.zeros((8, 128), F32))
    cfg = (chunk, seqs, first, last, length, tile, parts, cols, dim, wide, units, rank, sizes, len(sources))
    ANY = pl.BlockSpec(memory_space=pl.ANY)
    VM = pl.BlockSpec(memory_space=pltpu.VMEM)
    operands = [scal, *whole_rows, *received, gain, shift, b_qkv, b_up, rope, *weights, f_split, *sources, *acc]
    specs = [pl.BlockSpec(memory_space=pltpu.SMEM)] + [ANY] * (2 * parts) + [VM] * 4 + [ANY] * (8 + len(sources))
    flops = 2 * seqs * length * (dim * (units * 4 + wide * 8 + rank * 12) + units * rank * 6 + length * wide * 12)
    out = jax.ShapeDtypeStruct((2, seqs * length, dim // 2), BF)
    if not last:
        sums = [acc_shape, res_shape]
    else:
        sums = [jax.ShapeDtypeStruct((rank, 4 * wide + 2 * units), BF)]
        if direct:
            sums += [jax.ShapeDtypeStruct((high, dp, ranks, 2 * folds * rank), BF)] * 2
            sums += [jax.ShapeDtypeStruct((high, rank, 2 * own_cols), BF)] * 2
        else:
            sums += [jax.ShapeDtypeStruct((2, dp, dim // dp, rank), BF), jax.ShapeDtypeStruct((2 * rank, dim), BF)]
    in_shape = (2, dp, dim // dp, rank)
    tall = lambda n, dtype: pltpu.VMEM((length, n), dtype)
    flat = lambda n, dtype: pltpu.VMEM((n, length), dtype)
    return pl.pallas_call(
        functools.partial(block_kernel, cfg),
        out_shape=[out, out, *sums],
        in_specs=specs,
        out_specs=[ANY] * (2 + len(sums)),
        scratch_shapes=[
            pltpu.VMEM(in_shape, BF),
            pltpu.VMEM(in_shape if last else (2, 1, 16, rank), BF),
            pltpu.VMEM((2 * rank, dim) if last else (16, 128), BF),
            pltpu.VMEM((rank, 4 * wide + 2 * units) if last else (16, 128), BF),
            pltpu.VMEM((2, length, dim), BF),
            pltpu.VMEM((2, length, dim), BF),
            pltpu.VMEM((dim + rank, 3 * wide + rank), BF),
            pltpu.VMEM((dim + rank, units + rank), BF),
            pltpu.VMEM((units + wide + 2 * rank, dim + 2 * rank), BF),
            pltpu.VMEM((rank, units + wide), BF),
            pltpu.VMEM(rope.shape, F32),
            pltpu.VMEM(acc_shape.shape, F32),
            pltpu.VMEM(res_shape.shape, F32),
            tall(wide, BF), tall(wide, BF), tall(wide, BF), tall(wide, BF),
            flat(wide, BF), flat(wide, BF),
            tall(wide, F32), flat(wide, F32), flat(wide, F32),
            tall(units + wide, BF), tall(dim, F32),
            flat(rank, BF), flat(rank, BF),
            pltpu.VMEM((2, length, dim), BF),
            pltpu.SemaphoreType.DMA((2, steps, 2 * parts)),
            pltpu.SemaphoreType.DMA((8 + (4 * high * (folds + 1) if direct else 3),)),
            pltpu.SemaphoreType.DMA((steps, 2 * parts)),
            pltpu.SemaphoreType.DMA((5 + 4 * high * (folds + 1),)),
        ],
        input_output_aliases={} if first or last else {len(operands) - 2: 2, len(operands) - 1: 3},
        compiler_params=pltpu.CompilerParams(vmem_limit_bytes=60 * 1024 * 1024),
        cost_estimate=pl.CostEstimate(
            flops=2 * flops, bytes_accessed=32 * 1024 * 1024, transcendentals=2 * seqs * length * units
        ),
        name="block",
    )(*operands)


def finish_kernel(cfg, lens, *refs):
    terms, block, length, aliased = cfg
    parts, refs = refs[:terms], refs[terms:]
    tokens, cotangent, bias = refs[:3]
    result, grad = refs[-2:]
    at = pl.program_id(0) * block
    seq_len = lens[at // length]
    position = at % length + lax.broadcasted_iota(jnp.int32, (block, 1), 0)
    valid = position < seq_len
    total = sum(part[...].astype(F32) for part in parts)
    result[...] = jnp.where(valid, tokens[...].astype(F32) + total[0] + bias[0:1, :] + bias[1:2, :], 0.0)
    grad[...] = jnp.where(valid, cotangent[...].astype(F32) + total[1], 0.0)


def finish_call(chunk, lens, parts, tokens, cotangent, bias, length, earlier):
    rows, cols = tokens.shape
    span = parts[0].shape[1]
    block = min(512, length)
    base = chunk * span // block
    part_spec = pl.BlockSpec((2, block, cols), lambda i: (0, i, 0))
    row_spec = pl.BlockSpec((block, cols), lambda i: (base + i, 0))
    specs = [pl.BlockSpec(memory_space=pltpu.SMEM)] + [part_spec] * len(parts) + [row_spec] * 2
    specs += [pl.BlockSpec(bias.shape, lambda i: (0, 0))] + [pl.BlockSpec(memory_space=pl.ANY)] * len(earlier)
    operands = [lens, *parts, tokens, cotangent, bias, *earlier]
    return pl.pallas_call(
        functools.partial(finish_kernel, (len(parts), block, length, bool(earlier))),
        grid=(span // block,),
        out_shape=[jax.ShapeDtypeStruct((rows, cols), F32)] * 2,
        in_specs=specs,
        out_specs=[row_spec] * 2,
        input_output_aliases={len(operands) - 2: 0, len(operands) - 1: 1} if earlier else {},
        cost_estimate=pl.CostEstimate(flops=8 * span * cols, bytes_accessed=20 * span * cols, transcendentals=0),
        name="finish",
    )(*operands)


def merge_kernel(cfg, scal, *refs):
    sizes, dim, wide, units, rank, n_src, cut = cfg
    (w_qkv, w_up, w_down, w_out, f_split), refs = refs[:5], refs[5:]
    sources, refs = refs[:n_src], refs[n_src:]
    outs, refs = refs[:4], refs[4:]
    weights_v, outs_v, (fin_v, res0_v, res1_v, split_v, t_v, in_sems, out_sems) = refs[:4], refs[4:8], refs[8:]
    core = lax.rem(scal[0], 2)
    pairs = input_pairs(sizes, core, sources, fin_v, (res0_v, res1_v)) + [(f_split, split_v)]
    pairs += list(zip((w_qkv, w_up, w_down, w_out), weights_v))
    loads = [pltpu.make_async_copy(a, b, in_sems.at[i]) for i, (a, b) in enumerate(pairs)]
    for load in loads:
        load.start()
    for load in loads:
        load.wait()
    mixed = 3 * wide
    t_v[...] = split_v[:, mixed + units :].astype(F32).T.astype(BF)
    plans = [
        (0, dim, lambda rows: fin_v[0].reshape(dim, rank)[rows], lambda: split_v[:, :mixed]),
        (1, dim, lambda rows: fin_v[1].reshape(dim, rank)[rows], lambda: split_v[:, mixed : mixed + units]),
        (2, units, lambda rows: t_v[rows, :], lambda: res1_v[...]),
        (3, wide, lambda rows: t_v[units + rows.start : units + rows.stop, :], lambda: res0_v[...]),
    ]
    stores = []
    for which, depth, left, right in plans:
        for at in range(0, depth, cut):
            rows = slice(at, at + cut)
            outs_v[which][rows, :] = weights_v[which][rows, :].astype(F32) + mm(left(rows), right())
            copy = pltpu.make_async_copy(outs_v[which].at[rows, :], outs[which].at[rows, :], out_sems.at[len(stores)])
            copy.start()
            stores.append(copy)
    for copy in stores:
        copy.wait()


def merge_call(scal, weights, f_split, sources, sizes, dp):
    w_qkv, w_up, w_down, w_out = weights
    dim, units, wide, rank = w_up.shape[0], w_up.shape[1], w_out.shape[0], f_split.shape[0]
    high, folds, ranks, _, own_cols, direct = sizes
    cut = min(256, wide)
    ANY = pl.BlockSpec(memory_space=pl.ANY)
    chunks = (2 * dim + units + wide) // cut
    return pl.pallas_call(
        functools.partial(merge_kernel, (sizes, dim, wide, units, rank, len(sources), cut)),
        out_shape=[jax.ShapeDtypeStruct(w.shape, F32) for w in weights],
        in_specs=[pl.BlockSpec(memory_space=pltpu.SMEM)] + [ANY] * (5 + len(sources)),
        out_specs=[ANY] * 4,
        scratch_shapes=[pltpu.VMEM(w.shape, BF) for w in weights]
        + [pltpu.VMEM(w.shape, F32) for w in weights]
        + [
            pltpu.VMEM((2, dp, dim // dp, rank), BF),
            pltpu.VMEM((rank, dim), BF),
            pltpu.VMEM((rank, dim), BF),
            pltpu.VMEM(f_split.shape, BF),
            pltpu.VMEM((units + wide, rank), BF),
            pltpu.SemaphoreType.DMA((5 + (4 * high * (folds + 1) if direct else 3),)),
            pltpu.SemaphoreType.DMA((chunks,)),
        ],
        compiler_params=pltpu.CompilerParams(vmem_limit_bytes=40 * 1024 * 1024),
        cost_estimate=pl.CostEstimate(
            flops=2 * rank * (dim * (3 * wide + 2 * units + wide)), bytes_accessed=20 * 1024 * 1024, transcendentals=0
        ),
        name="merge",
    )(scal, *weights, f_split, *sources)


def bits_of(size):
    return [1 << b for b in range(size.bit_length() - 1)]


def swap(x, axis, size, bit):
    return lax.ppermute(x, axis, [(i, i ^ bit) for i in range(size)])


def bit_value(axis, bit):
    return (lax.axis_index(axis) // bit) % 2


def halve(x, axis, size, bit):
    mine = bit_value(axis, bit)
    keep = lax.dynamic_index_in_dim(x, mine, 0, keepdims=False).astype(F32)
    give = lax.dynamic_index_in_dim(x, 1 - mine, 0, keepdims=False).astype(BF)
    return keep + swap(give, axis, size, bit).astype(F32)


def after(x, *earlier):
    return lax.optimization_barrier((x, earlier))[0]


def in_order(x, other, axis, bit):
    upper = bit_value(axis, bit) == 1
    return jnp.where(upper, other, x), jnp.where(upper, x, other)


def spread_inputs(low_in, low_res, mp, wait=()):
    own_rows, rank = low_in.shape[1:]
    own_ranks = low_res.shape[1]
    both = jnp.concatenate(
        [low_in[n, j * own_ranks : (j + 1) * own_ranks] for n in range(2) for j in range(own_rows // own_ranks)]
        + [low_res[0], low_res[1]],
        1,
    )
    if wait:
        both = after(both, *wait)
    for bit in bits_of(mp)[1:]:
        both = jnp.concatenate(in_order(both, swap(both, "mp", mp, bit), "mp", bit), 1)
    return both


def gather_rows(x, dp):
    found = lax.all_to_all(jnp.broadcast_to(x[None], (dp,) + x.shape), "dp", 0, 0, tiled=True)
    return found.reshape(dp * x.shape[0], x.shape[1])


def gather_inputs(both, sizes, dim, dp, mp):
    high, folds, ranks, rank, own_cols, direct = sizes
    found = gather_rows(both, dp)
    other = swap(found, "mp", mp, 1)
    if direct:
        deep = lambda x: x.reshape(dp, ranks, x.shape[1])
        return [deep(found), deep(other), found, other]
    cores = jnp.stack(in_order(found, other, "mp", 1)).reshape(2, dp, ranks, high, both.shape[1] // high)
    in_part = cores[..., : 2 * folds * rank].reshape(2, dp, ranks, high, 2, folds, rank)
    res_part = cores[..., 2 * folds * rank :].reshape(2, dp, ranks, high, 2, own_cols)
    whole_in = in_part.transpose(4, 1, 3, 0, 5, 2, 6).reshape(2, dp, dim // dp, rank)
    return [whole_in, res_part.transpose(4, 1, 2, 3, 0, 5).reshape(2, rank, dim)]


def reduce_inputs(sums, sizes, dim, dp, mp):
    high, folds, ranks, rank, own_cols, direct = sizes
    if direct:
        in_keep, in_send, res_keep, res_send = sums
        in_both = in_keep.astype(F32) + swap(in_send, "mp", mp, 1).astype(F32)
        res_both = res_keep.astype(F32) + swap(res_send, "mp", mp, 1).astype(F32)
        both = jnp.concatenate([in_both.reshape(high, rank, -1), res_both], 2)
    else:
        in_part = sums[0].reshape(2, dp, high, 2, folds, ranks, rank)
        in_part = in_part.transpose(3, 2, 1, 5, 0, 4, 6).reshape(2, high, rank, 2 * folds * rank)
        res_part = sums[1].reshape(2, rank, high, 2, own_cols).transpose(3, 2, 1, 0, 4)
        both = halve(jnp.concatenate([in_part, res_part.reshape(2, high, rank, 2 * own_cols)], 3), "mp", mp, 1)
    both = both.reshape((2,) * len(bits_of(high)) + both.shape[1:])
    for bit in reversed(bits_of(mp)[1:]):
        both = halve(both, "mp", mp, bit)
    return both


def reduce_rows(x, dp):
    return jnp.sum(lax.all_to_all(x.reshape(dp, -1, x.shape[1]), "dp", 0, 0, tiled=True).astype(F32), 0)


def adam_step(factor, moment, gradient):
    first_moment = 0.9 * moment[0] + 0.1 * gradient
    second_moment = 0.999 * moment[1] + 0.001 * gradient * gradient
    updated = factor - 0.01 * (first_moment / first_fix) / (
        jnp.sqrt(second_moment / second_fix) + 1e-08
    )
    keep_mask = (jnp.abs(moment[0]) >= 0.5).astype(F32)
    return (updated, jnp.stack([first_moment * keep_mask, second_moment * keep_mask]))


def rope_tables(length):
    half = ROT // 2
    frequency = 10000.0 ** (-jnp.arange(half, dtype=F32) * 2.0 / ROT)
    angles = jnp.arange(length, dtype=F32)[:, None] * frequency[None, :]
    cos, sin = jnp.cos(angles), jnp.sin(angles)
    ones, zeros = jnp.ones((length, HEAD - ROT), F32), jnp.zeros((length, HEAD - ROT), F32)
    blank = jnp.zeros_like(sin)
    one_head = [
        jnp.concatenate([cos, cos, ones], 1),
        jnp.concatenate([-sin, blank, zeros], 1),
        jnp.concatenate([blank, sin, zeros], 1),
    ]
    return jnp.stack([jnp.concatenate([table, table], 1) for table in one_head])


def per_device(
    dp,
    mp,
    tokens,
    cotangent,
    lengths,
    norm_gain,
    norm_shift,
    qkv_weight,
    out_weight,
    up_weight,
    down_weight,
    qkv_bias,
    up_bias,
    res_bias,
    in_factor,
    qkv_factor,
    up_factor,
    out_factor,
    down_factor,
    res_factor,
    in_moments,
    qkv_moments,
    up_moments,
    out_moments,
    down_moments,
    res_moments,
):
    row_count, cols = tokens.shape
    seq_count = lengths.shape[0]
    length = row_count // seq_count
    wide = out_weight.shape[0]
    dim, units = up_weight.shape
    me = lax.axis_index("mp").astype(jnp.int32)
    mp_bits = bits_of(mp)
    seqs = 2 if seq_count % 2 == 0 else 1
    chunks = seq_count // seqs
    span = seqs * length

    rank = in_factor.shape[2]
    low = lambda f: f.astype(BF)
    both = spread_inputs(low(in_factor), low(res_factor), mp)

    own_ranks, own_cols = res_factor.shape[1:]
    sizes = (mp // 2, in_factor.shape[1] // own_ranks, own_ranks, rank, own_cols, own_ranks % 16 == 0)
    rank_rows = lambda qkv, up, down, out: jnp.concatenate([low(qkv), low(up), low(down).T, low(out).T], 1)
    f_split = gather_rows(rank_rows(qkv_factor, up_factor, down_factor, out_factor), dp)
    sources = gather_inputs(both, sizes, dim, dp, mp)
    whole_rows = (tokens, cotangent, swap(tokens, "mp", mp, 1), swap(cotangent, "mp", mp, 1))

    def far_rows(c, wait):
        held = {0: [tokens[c * span : (c + 1) * span], cotangent[c * span : (c + 1) * span]]}
        for bit in reversed(mp_bits[1:]):
            for k in list(held):
                held[k | bit] = [swap(after(x, *wait), "mp", mp, bit) for x in held[k]]
        return {k: v for k, v in held.items() if k}

    def near_rows(held, wait):
        for k in list(held):
            held[k | 1] = [swap(after(x, *wait) if wait else x, "mp", mp, 1) for x in held[k]]
        return [x for k in sorted(held) for x in held[k]]

    small = (norm_gain, norm_shift, qkv_bias[None], up_bias[None], rope_tables(length))
    marks = [3 * wide, 3 * wide + units, 3 * wide + 2 * units]

    def pieces(packed):
        return jnp.split(packed, marks, 1)

    weights = (qkv_weight, up_weight, down_weight, out_weight)

    def near_sums(keep, send):
        other = swap(send, "mp", mp, 1)
        column = lambda x, j: x[:, :, j * cols : (j + 1) * cols]
        held = {2 * j: [column(keep, j), column(other, j)] for j in range(mp // 2)}
        held[0] = [keep, other]
        return held

    def far_gives(held, bit):
        gone = [k for k in held if k & bit]
        return gone, jnp.concatenate([sum(x.astype(F32) for x in held[k]).astype(BF) for k in gone], 0)

    def far_sums(held, first_give, wait):
        for bit in mp_bits[1:]:
            gone, give = first_give if bit == 2 else far_gives(held, bit)
            moved = swap(after(give, *wait) if wait else give, "mp", mp, bit)
            wait = (moved,)
            for j, k in enumerate(gone):
                held[k ^ bit].append(moved[2 * j : 2 * j + 2])
                del held[k]
        return held[0], wait

    acc = None
    partials, totals = [], []
    far = far_rows(0, (both,))
    for c in range(chunks):
        scal = jnp.concatenate([lengths[c * seqs : (c + 1) * seqs], me[None]])
        wait = () if c == 0 else (partials[-1][0],)
        received = near_rows(far, wait)
        if c + 1 < chunks:
            far = far_rows(c + 1, (received[-1], sources[-1], f_split))
        keep, send, *acc = block_call(
            c, seqs, c == chunks - 1, sizes, acc, scal, whole_rows, received, small, weights,
            (f_split, sources), length, mp,
        )
        partials.append((keep, send))

    split_sum, *input_sums = acc
    grads_both = reduce_inputs(input_sums, sizes, dim, dp, mp)
    wait = (grads_both,)
    for c in range(chunks - 1):
        held = near_sums(*partials[c])
        give = far_gives(held, 2)
        split_sum = after(split_sum, give[1])
        total, wait = far_sums(held, give, wait)
        totals.append(total)
    split_grad = reduce_rows(split_sum, dp)
    own_both = reduce_rows(grads_both.astype(BF), dp)
    own_both, split_grad = after((own_both, split_grad), *wait)
    held = near_sums(*partials[-1])
    last_give = far_gives(held, 2)
    cut = own_both.shape[1] - 2 * own_cols
    in_grad = own_both[:, :cut].reshape(own_ranks, 2, -1, rank).transpose(1, 2, 0, 3).reshape(in_factor.shape)
    res_grad = jnp.stack([own_both[:, cut : cut + own_cols], own_both[:, cut + own_cols :]])
    qkv_owned, up_owned, down_owned, out_owned = pieces(split_grad)
    down_owned, out_owned = down_owned.T, out_owned.T
    new_in, in_pruned = adam_step(in_factor, in_moments, in_grad)
    new_qkv, qkv_pruned = adam_step(qkv_factor, qkv_moments, qkv_owned)
    new_up, up_pruned = adam_step(up_factor, up_moments, up_owned)
    new_out, out_pruned = adam_step(out_factor, out_moments, out_owned)
    new_down, down_pruned = adam_step(down_factor, down_moments, down_owned)
    new_res, res_pruned = adam_step(res_factor, res_moments, res_grad)
    both = spread_inputs(low(new_in), low(new_res), mp)
    total, _ = far_sums(held, last_give, (both,))
    totals.append(total)
    split_whole = gather_rows(rank_rows(new_qkv, new_up, new_down, new_out), dp)
    merged_qkv, merged_up, merged_down, merged_out = merge_call(
        me[None], weights, split_whole, gather_inputs(both, sizes, dim, dp, mp), sizes, dp
    )
    ended = []
    for c in range(chunks):
        ended = finish_call(
            c, lengths[c * seqs : (c + 1) * seqs], totals[c], tokens, cotangent, res_bias, length, ended
        )
    result, grad_tokens = ended
    return (
        result,
        grad_tokens,
        in_grad,
        qkv_owned,
        up_owned,
        out_owned,
        down_owned,
        res_grad,
        merged_qkv,
        merged_out,
        merged_up,
        merged_down,
        in_pruned,
        qkv_pruned,
        up_pruned,
        out_pruned,
        down_pruned,
        res_pruned,
    )


def solution(mesh):
    placed = (
        P("dp", "mp"),
        P("dp", "mp"),
        P("dp"),
        P(),
        P(),
        P(None, "mp"),
        P("mp", None),
        P(None, "mp"),
        P("mp", None),
        P("mp"),
        P("mp"),
        P(None, "mp"),
        P(None, ("dp", "mp"), None),
        P("dp", "mp"),
        P("dp", "mp"),
        P("mp", "dp"),
        P("mp", "dp"),
        P(None, "dp", "mp"),
        P(None, None, ("dp", "mp"), None),
        P(None, "dp", "mp"),
        P(None, "dp", "mp"),
        P(None, "mp", "dp"),
        P(None, "mp", "dp"),
        P(None, None, "dp", "mp"),
    )
    return jax.shard_map(
        functools.partial(per_device, mesh.shape["dp"], mesh.shape["mp"]),
        mesh=mesh,
        in_specs=placed,
        out_specs=(
            P("dp", "mp"),
            P("dp", "mp"),
            P(None, ("dp", "mp"), None),
            P("dp", "mp"),
            P("dp", "mp"),
            P("mp", "dp"),
            P("mp", "dp"),
            P(None, "dp", "mp"),
            P(None, "mp"),
            P("mp", None),
            P(None, "mp"),
            P("mp", None),
            P(None, None, ("dp", "mp"), None),
            P(None, "dp", "mp"),
            P(None, "dp", "mp"),
            P(None, "mp", "dp"),
            P(None, "mp", "dp"),
            P(None, None, "dp", "mp"),
        ),
        check_vma=False,
    )
```

```python
import functools
import math

import jax
import jax.numpy as jnp
import numpy as np
from jax import lax
from jax.experimental import pallas as pl
from jax.experimental.pallas import tpu as pltpu
from jax.sharding import PartitionSpec as P

HEAD = 64
ROT = 16
BF = jnp.bfloat16
F32 = jnp.float32

first_fix = 1.0 - math.exp(100.0 * math.log(0.9))
second_fix = 1.0 - math.exp(100.0 * math.log(0.999))


def mm(a, b):
    return lax.dot_general(a, b, (((1,), (0,)), ((), ())), preferred_element_type=F32)


def mm_t(a, b):
    return lax.dot_general(a, b, (((1,), (1,)), ((), ())), preferred_element_type=F32)


def rows_mm(a, b):
    return lax.dot_general(a, b, (((0,), (0,)), ((), ())), preferred_element_type=F32)


def layer_norm(x):
    centred = x - jnp.mean(x, -1, keepdims=True)
    scale = lax.rsqrt(jnp.mean(centred * centred, -1, keepdims=True) + 1e-05)
    return centred * scale, scale


def layer_norm_back(grad_unit, unit_rows, scale):
    return scale * (
        grad_unit
        - jnp.mean(grad_unit, -1, keepdims=True)
        - unit_rows * jnp.mean(grad_unit * unit_rows, -1, keepdims=True)
    )


def rotate(values, cos, sin_a, sin_b, sign):
    width = values.shape[-1]
    turned = pltpu.roll(values, width - ROT // 2, 1) * sin_a + pltpu.roll(values, ROT // 2, 1) * sin_b
    return values * cos + turned if sign > 0 else values * cos - turned


def input_pairs(sizes, core, sources, fin_v, res_places):
    high, folds, ranks, rank, own_cols, direct = sizes
    if not direct:
        f_in, f_res = sources
        return [(f_in, fin_v), (f_res.at[0], res_places[0]), (f_res.at[1], res_places[1])]
    width = 2 * folds * rank + 2 * own_cols
    found = []
    for c in range(2):
        deep, wide2 = sources[c], sources[2 + c]
        which = core if c == 0 else 1 - core
        for y in range(high):
            for n in range(2):
                for j in range(folds):
                    at = y * width + (n * folds + j) * rank
                    rows = pl.ds(pl.multiple_of(((y * 2 + which) * folds + j) * ranks, ranks), ranks)
                    found.append((deep.at[:, :, at : at + rank], fin_v.at[n, :, rows, :]))
                at = y * width + 2 * folds * rank + n * own_cols
                place = pl.ds(pl.multiple_of((y * 2 + which) * own_cols, own_cols), own_cols)
                found.append((wide2.at[:, at : at + own_cols], res_places[n].at[:, place]))
    return found


def block_kernel(cfg, scal, *refs):
    chunk, seqs, first, last, length, tile, parts, cols, dim, wide, units, rank, sizes, n_src = cfg
    whole_rows, refs = refs[:4], refs[4:]
    received, refs = refs[: 2 * parts - 4], refs[2 * parts - 4 :]
    (gain, shift, b_qkv, b_up, rope, w_qkv, w_up, w_down, w_out, f_split), refs = refs[:10], refs[10:]
    sources, refs = refs[:n_src], refs[n_src:]
    (acc_in, res_in), refs = refs[:2], refs[2:]
    outs, refs = refs[: 2 * parts], refs[2 * parts :]
    sums, refs = refs[: len(refs) - 31], refs[len(refs) - 31 :]
    (
        fin_v, gin_b, gres_b, gsplit_b, x_v, c_v, wq_v, wu_v, wd_v, ft_v, rope_v, acc_v, res_v,
        q_s, k_s, v_s, g_s, qt_s, gt_s, gq_s, gkt_s, gvt_s, ac_s, p_s, qr_s, gor_s, out_v,
        row_sems, w_sems, out_sems, acc_sems,
    ) = refs
    me = scal[seqs]
    core = lax.rem(me, 2)
    steps = length // tile
    mixed_cols = 3 * wide
    joint = units + wide
    skip = f_split.shape[1] - mixed_cols - units - joint

    def tiles_of(s):
        return (scal[s] + tile - 1) // tile

    def row_slice(t, size=tile):
        return pl.ds(pl.multiple_of(t * tile, tile), size)


    def row_copies(s, t):
        found = []
        slot = lax.rem(s, 2)
        for which, dest in enumerate((x_v, c_v)):
            for k in range(parts):
                at = pl.ds(pl.multiple_of(s * length + t * tile, tile), tile)
                if k < 2:
                    src = whole_rows[2 * k + which].at[
                        pl.ds(pl.multiple_of((chunk + s) * length + t * tile, tile), tile), :
                    ]
                else:
                    src = received[2 * (k - 2) + which].at[at, :]
                place = pl.ds(pl.multiple_of(jnp.bitwise_xor(me, k) * cols, cols), cols)
                found.append(
                    pltpu.make_async_copy(
                        src, dest.at[slot, row_slice(t), place], row_sems.at[slot, t, which * parts + k]
                    )
                )
        return found

    def start_rows(s):
        def one(t, carry):
            for copy in row_copies(s, t):
                copy.start()
            return carry

        lax.fori_loop(0, tiles_of(s), one, 0)

    def out_copies(s, t):
        found = []
        for which in range(2):
            for k in range(parts):
                place = pl.ds(pl.multiple_of(jnp.bitwise_xor(me, k) * cols, cols), cols)
                rows = pl.ds(pl.multiple_of(s * length + t * tile, tile), tile)
                found.append(
                    pltpu.make_async_copy(
                        out_v.at[which, row_slice(t), place],
                        outs[2 * k + which].at[rows, :],
                        out_sems.at[t, which * parts + k],
                    )
                )
        return found

    def drain(s):
        def one(t, carry):
            for copy in out_copies(s, t):
                copy.wait()
            return carry

        lax.fori_loop(0, tiles_of(s), one, 0)

    res_places = (wd_v.at[joint + rank :, :dim], wd_v.at[joint : joint + rank, :dim])
    pairs = [
        (w_qkv, wq_v.at[:dim, :mixed_cols]),
        (f_split.at[:, skip : skip + mixed_cols], wq_v.at[dim:, :mixed_cols]),
        (rope, rope_v),
        (w_up, wu_v.at[:dim, :units]),
        (f_split.at[:, skip + mixed_cols : skip + mixed_cols + units], wu_v.at[dim:, :units]),
        (w_down, wd_v.at[:units, :dim]),
        (w_out, wd_v.at[units:joint, :dim]),
        (f_split.at[:, skip + mixed_cols + units :], ft_v),
    ] + input_pairs(sizes, core, sources, fin_v, res_places)
    loads = [pltpu.make_async_copy(a, b, w_sems.at[i]) for i, (a, b) in enumerate(pairs)]
    start_rows(0)
    for load in loads:
        load.start()
    back_in = []
    if first:
        acc_v[...] = jnp.zeros_like(acc_v)
        res_v[...] = jnp.zeros_like(res_v)
    else:
        back_in = [
            pltpu.make_async_copy(acc_in, acc_v, acc_sems.at[0]),
            pltpu.make_async_copy(res_in, res_v, acc_sems.at[1]),
        ]
        for copy in back_in:
            copy.start()
    wd_v[:units, dim + rank :] = jnp.zeros((units, rank), BF)
    wd_v[units:joint, dim : dim + rank] = jnp.zeros((wide, rank), BF)
    for load in loads:
        load.wait()
    for copy in back_in:
        copy.wait()
    wd_v[:units, dim : dim + rank] = ft_v[:, :units].astype(F32).T.astype(BF)
    wd_v[units:joint, dim + rank :] = ft_v[:, units:].astype(F32).T.astype(BF)
    wq_v[:dim, mixed_cols:] = fin_v[0].reshape(dim, rank)
    wu_v[:dim, units:] = fin_v[1].reshape(dim, rank)

    def whole(ref, top, depth, width, cut, other, at):
        def one(i, carry):
            rows = pl.ds(pl.multiple_of(top + i * cut, cut), cut)
            low_rank = mm(ref[rows, at : at + rank], other())
            ref[rows, :width] = (ref[rows, :width].astype(F32) + low_rank).astype(BF)
            return carry

        lax.fori_loop(0, depth // cut, one, 0)

    cut = min(256, units, wide)
    whole(wu_v, 0, dim, units, cut, lambda: wu_v[dim:, :units], units)
    whole(wd_v, 0, units, dim, cut, lambda: wd_v[joint : joint + rank, :dim], dim)
    whole(wd_v, units, wide, dim, cut, lambda: wd_v[joint + rank :, :dim], dim + rank)

    c_in0, c_in1, c_qkv, c_up, c_down, c_out = (
        slice(0, dim),
        slice(dim, 2 * dim),
        slice(2 * dim, 2 * dim + mixed_cols),
        slice(2 * dim + mixed_cols, 2 * dim + mixed_cols + units),
        slice(2 * dim + mixed_cols + units, 2 * dim + mixed_cols + 2 * units),
        slice(2 * dim + mixed_cols + 2 * units, 2 * dim + mixed_cols + 2 * units + wide),
    )
    lane = lax.broadcasted_iota(jnp.int32, (1, 128), 1)
    left = lane < HEAD

    def one_sequence(s, carry):
        seq_len = scal[s]
        count = tiles_of(s)
        slot = lax.rem(s, 2)

        @pl.when(s + 1 < seqs)
        def _():
            start_rows(s + 1)

        gkt_s[...] = jnp.zeros_like(gkt_s)
        gvt_s[...] = jnp.zeros_like(gvt_s)

        def upstream(t, size):
            position = t * tile + lax.broadcasted_iota(jnp.int32, (size, 1), 0)
            return jnp.where(position < seq_len, c_v[slot, row_slice(t, size), :].astype(F32), 0.0).astype(BF)

        def tables(t, size):
            rows = row_slice(t, size)
            return [jnp.concatenate([rope_v[i, rows, :]] * (wide // 128), 1) for i in range(3)]

        def forward(t, size):
            rows = row_slice(t, size)
            for j in range(size // tile):
                for copy in row_copies(s, t + j):
                    copy.wait()
            unit, _ = layer_norm(x_v[slot, rows, :].astype(F32))
            low_one = (unit * gain[0:1, :] + shift[0:1, :]).astype(BF)
            low_two = (unit * gain[1:2, :] + shift[1:2, :]).astype(BF)
            ups = upstream(t, size)
            hidden = mm(low_two, wu_v[:dim, :])
            back = mm_t(ups, wd_v[:, :dim])
            mixed = mm(low_one, wq_v[:dim, :])
            code_up = hidden[:, units:]
            hidden = hidden[:, :units] + b_up[...]
            code_qkv = mixed[:, mixed_cols:]
            mixed = mixed[:, :mixed_cols] + mm(code_qkv.astype(BF), wq_v[dim:, :mixed_cols]) + b_qkv[...]
            blocks = [mixed[:, i * 128 : (i + 1) * 128] for i in range(mixed_cols // 128)]
            cat = lambda found: jnp.concatenate(found, 1) if len(found) > 1 else found[0]
            q_mixed = cat([jnp.where(left, blocks[3 * p], blocks[3 * p + 1]) for p in range(wide // 128)])
            k_mixed = cat(
                [pltpu.roll(jnp.where(left, blocks[3 * p + 2], blocks[3 * p]), HEAD, 1) for p in range(wide // 128)]
            )
            v_mixed = cat([jnp.where(left, blocks[3 * p + 1], blocks[3 * p + 2]) for p in range(wide // 128)])
            cdf = 0.5 * (1.0 + lax.erf(hidden * (1.0 / math.sqrt(2.0))))
            active = (hidden * cdf).astype(BF)
            slope = cdf + hidden * (jnp.exp(-0.5 * hidden * hidden) * (1.0 / math.sqrt(2.0 * math.pi)))
            grad_hidden = (back[:, :units] * slope).astype(BF)
            ac_s[rows, :units] = active
            cos, sin_a, sin_b = tables(t, size)
            query = rotate(q_mixed, cos, sin_a, sin_b, 1).astype(BF).astype(F32) * HEAD**-0.5
            q_s[rows, :] = query.astype(BF)
            qt_s[:, rows] = query.T.astype(BF)
            k_s[rows, :] = rotate(k_mixed, cos, sin_a, sin_b, 1).astype(BF)
            v_s[rows, :] = v_mixed.astype(BF)
            qr_s[:, rows] = code_qkv.T.astype(BF)
            grad_context = back[:, units:joint]
            g_s[rows, :] = grad_context.astype(BF)
            gt_s[:, rows] = grad_context.T.astype(BF)
            gor_s[:, rows] = back[:, joint + rank :].T.astype(BF)
            below = mm_t(grad_hidden, wu_v[:, :units])
            p_s[rows, :] = below[:, :dim] * gain[1:2, :]
            acc_v[:, c_up] += mm(code_up.T.astype(BF), grad_hidden)
            acc_v[:, c_down] += mm(back[:, joint : joint + rank].T.astype(BF), active)
            acc_v[:, c_in1] += mm(below[:, dim:].T.astype(BF), low_two)

        def finish(t, size):
            rows = row_slice(t, size)
            cos, sin_a, sin_b = tables(t, size)
            grad_q = rotate(gq_s[rows, :], cos, sin_a, sin_b, -1)
            grad_k = rotate(gkt_s[:, rows].T, cos, sin_a, sin_b, -1)
            grad_v = gvt_s[:, rows].T
            blocks = []
            for p in range(wide // 128):
                pair = slice(p * 128, (p + 1) * 128)
                one_q, one_k, one_v = grad_q[:, pair], pltpu.roll(grad_k[:, pair], HEAD, 1), grad_v[:, pair]
                blocks += [jnp.where(left, one_q, one_k), jnp.where(left, one_v, one_q), jnp.where(left, one_k, one_v)]
            grad_mixed = jnp.concatenate(blocks, 1).astype(BF)
            below = mm_t(grad_mixed, wq_v[:, :mixed_cols])
            both = ac_s[rows, :]
            ahead = mm(both, wd_v[:joint, :])
            unit, scale = layer_norm(x_v[slot, rows, :].astype(F32))
            low_one = (unit * gain[0:1, :] + shift[0:1, :]).astype(BF)
            out_v[0, rows, :] = ahead[:, :dim].astype(BF)
            grad_code = below[:, dim:]
            grad_norm = below[:, :dim] + mm_t(grad_code.astype(BF), wq_v[:dim, mixed_cols:])
            grad_unit = grad_norm * gain[0:1, :] + p_s[rows, :]
            out_v[1, rows, :] = layer_norm_back(grad_unit, unit, scale).astype(BF)
            for j in range(size // tile):
                for copy in out_copies(s, t + j):
                    copy.start()
            acc_v[:, c_in0] += mm(grad_code.T.astype(BF), low_one)
            acc_v[:, c_qkv] += mm(qr_s[:, rows], grad_mixed)
            acc_v[:, c_out] += mm(gor_s[:, rows], both[:, units:])
            res_v[...] += mm(ahead[:, dim:].T.astype(BF), upstream(t, size))

        def over_rows(work):
            def single(j, carry):
                work(j, tile)
                return carry

            lax.fori_loop(0, count, single, 0)

        over_rows(forward)

        for i in range(steps):
            @pl.when(i < count)
            def _(i=i):
                qrows = pl.ds(i * tile, tile)
                before, extent = i * tile, (i + 1) * tile
                qpos = before + lax.broadcasted_iota(jnp.int32, (tile, tile), 0)
                kpos = before + lax.broadcasted_iota(jnp.int32, (tile, tile), 1)
                allowed = (kpos <= qpos) & (kpos < seq_len)
                allowed = jnp.concatenate([allowed, allowed], 0)
                def one_pair(p, carry):
                    pair = pl.ds(pl.multiple_of(p * 128, 128), 128)
                    q_all, g_all = q_s[qrows, pair], g_s[qrows, pair]
                    zero = jnp.zeros_like(q_all)
                    q_two = jnp.concatenate([jnp.where(left, q_all, zero), jnp.where(left, zero, q_all)], 0)
                    g_two = jnp.concatenate([jnp.where(left, g_all, zero), jnp.where(left, zero, g_all)], 0)
                    keys, vals = k_s[:extent, pair], v_s[:extent, pair]
                    scores = mm_t(q_two, keys)
                    grad_probs = mm_t(g_two, vals)
                    last = jnp.where(allowed, scores[:, before:], -1e30)
                    scores = jnp.concatenate([scores[:, :before], last], 1) if i else last
                    weights = jnp.exp(scores - jnp.max(scores, -1, keepdims=True))
                    probs = weights * (1.0 / jnp.sum(weights, -1, keepdims=True))
                    low_probs = probs.astype(BF)
                    context = mm(low_probs, vals)
                    row_term = jnp.sum(probs * grad_probs, -1, keepdims=True)
                    grad_scores = (probs * (grad_probs - row_term)).astype(BF)
                    grad_q = mm(grad_scores, keys)
                    ac_s[qrows, pl.ds(pl.multiple_of(units + p * 128, 128), 128)] = jnp.where(
                        left, context[:tile], context[tile:]
                    ).astype(BF)
                    gq_s[qrows, pair] = jnp.where(left, grad_q[:tile], grad_q[tile:]) * HEAD**-0.5
                    for h in range(2):
                        feats = pl.ds(pl.multiple_of(p * 128 + h * HEAD, HEAD), HEAD)
                        part = slice(h * tile, (h + 1) * tile)
                        gkt_s[feats, :extent] += mm(qt_s[feats, qrows], grad_scores[part])
                        gvt_s[feats, :extent] += mm(gt_s[feats, qrows], low_probs[part])
                    return carry

                lax.fori_loop(0, wide // 128, one_pair, 0)

        @pl.when(s > 0)
        def _():
            drain(s - 1)

        over_rows(finish)
        return carry

    lax.fori_loop(0, seqs, one_sequence, 0)
    if not last:
        targets = [(acc_v, sums[0]), (res_v, sums[1])]
    else:
        high, folds, ranks, _, own_cols, direct = sizes
        gsplit_b[...] = acc_v[:, 2 * dim :].astype(BF)
        gres_b[:rank, :] = res_v[rank:, :].astype(BF)
        gres_b[rank:, :] = res_v[:rank, :].astype(BF)
        for n, place in enumerate((c_in0, c_in1)):
            gin_b[n] = acc_v[:, place].T.astype(BF).reshape(gin_b.shape[1:])
        targets = [(gsplit_b, sums[0])]
        if not direct:
            targets += [(gin_b, sums[1]), (gres_b, sums[2])]
        else:
            for c in range(2):
                which = core if c == 0 else 1 - core
                for y in range(high):
                    for n in range(2):
                        for j in range(folds):
                            at = (n * folds + j) * rank
                            rows = pl.ds(pl.multiple_of(((y * 2 + which) * folds + j) * ranks, ranks), ranks)
                            targets.append((gin_b.at[n, :, rows, :], sums[1 + c].at[y, :, :, at : at + rank]))
                        place = pl.ds(pl.multiple_of((y * 2 + which) * own_cols, own_cols), own_cols)
                        targets.append(
                            (gres_b.at[n * rank : (n + 1) * rank, place],
                             sums[3 + c].at[y, :, n * own_cols : (n + 1) * own_cols])
                        )
    back_out = [pltpu.make_async_copy(a, b, acc_sems.at[2 + i]) for i, (a, b) in enumerate(targets)]
    for copy in back_out:
        copy.start()
    drain(seqs - 1)
    for copy in back_out:
        copy.wait()


def block_call(chunk, seqs, last, sizes, acc, scal, whole_rows, received, small, weights, factors, length, parts):
    gain, shift, b_qkv, b_up, rope = small
    w_qkv, w_up, w_down, w_out = weights
    f_split, sources = factors
    dim, units, wide, rank = w_up.shape[0], w_up.shape[1], w_out.shape[0], f_split.shape[0]
    high, folds, ranks, _, own_cols, direct = sizes
    dp = rank // ranks
    cols = dim // parts
    tile = 256 if length % 256 == 0 else 128
    steps = length // tile
    first = acc is None
    acc_shape = jax.ShapeDtypeStruct((rank, 2 * dim + 4 * wide + 2 * units), F32)
    res_shape = jax.ShapeDtypeStruct((2 * rank, dim), F32)
    if first:
        acc = (jnp.zeros((8, 128), F32), jnp.zeros((8, 128), F32))
    cfg = (chunk, seqs, first, last, length, tile, parts, cols, dim, wide, units, rank, sizes, len(sources))
    ANY = pl.BlockSpec(memory_space=pl.ANY)
    VM = pl.BlockSpec(memory_space=pltpu.VMEM)
    operands = [scal, *whole_rows, *received, gain, shift, b_qkv, b_up, rope, *weights, f_split, *sources, *acc]
    specs = [pl.BlockSpec(memory_space=pltpu.SMEM)] + [ANY] * (2 * parts) + [VM] * 4 + [ANY] * (8 + len(sources))
    flops = 2 * seqs * length * (dim * (units * 4 + wide * 8 + rank * 12) + units * rank * 6 + length * wide * 12)
    out = [jax.ShapeDtypeStruct((seqs * length, cols), BF)] * (2 * parts)
    if not last:
        sums = [acc_shape, res_shape]
    else:
        sums = [jax.ShapeDtypeStruct((rank, 4 * wide + 2 * units), BF)]
        if direct:
            sums += [jax.ShapeDtypeStruct((high, dp, ranks, 2 * folds * rank), BF)] * 2
            sums += [jax.ShapeDtypeStruct((high, rank, 2 * own_cols), BF)] * 2
        else:
            sums += [jax.ShapeDtypeStruct((2, dp, dim // dp, rank), BF), jax.ShapeDtypeStruct((2 * rank, dim), BF)]
    in_shape = (2, dp, dim // dp, rank)
    tall = lambda n, dtype: pltpu.VMEM((length, n), dtype)
    flat = lambda n, dtype: pltpu.VMEM((n, length), dtype)
    return pl.pallas_call(
        functools.partial(block_kernel, cfg),
        out_shape=[*out, *sums],
        in_specs=specs,
        out_specs=[ANY] * (2 * parts + len(sums)),
        scratch_shapes=[
            pltpu.VMEM(in_shape, BF),
            pltpu.VMEM(in_shape if last else (2, 1, 16, rank), BF),
            pltpu.VMEM((2 * rank, dim) if last else (16, 128), BF),
            pltpu.VMEM((rank, 4 * wide + 2 * units) if last else (16, 128), BF),
            pltpu.VMEM((2, length, dim), BF),
            pltpu.VMEM((2, length, dim), BF),
            pltpu.VMEM((dim + rank, 3 * wide + rank), BF),
            pltpu.VMEM((dim + rank, units + rank), BF),
            pltpu.VMEM((units + wide + 2 * rank, dim + 2 * rank), BF),
            pltpu.VMEM((rank, units + wide), BF),
            pltpu.VMEM(rope.shape, F32),
            pltpu.VMEM(acc_shape.shape, F32),
            pltpu.VMEM(res_shape.shape, F32),
            tall(wide, BF), tall(wide, BF), tall(wide, BF), tall(wide, BF),
            flat(wide, BF), flat(wide, BF),
            tall(wide, F32), flat(wide, F32), flat(wide, F32),
            tall(units + wide, BF), tall(dim, F32),
            flat(rank, BF), flat(rank, BF),
            pltpu.VMEM((2, length, dim), BF),
            pltpu.SemaphoreType.DMA((2, steps, 2 * parts)),
            pltpu.SemaphoreType.DMA((8 + (4 * high * (folds + 1) if direct else 3),)),
            pltpu.SemaphoreType.DMA((steps, 2 * parts)),
            pltpu.SemaphoreType.DMA((5 + 4 * high * (folds + 1),)),
        ],
        input_output_aliases={} if first or last else {len(operands) - 2: 2 * parts, len(operands) - 1: 2 * parts + 1},
        compiler_params=pltpu.CompilerParams(vmem_limit_bytes=60 * 1024 * 1024),
        cost_estimate=pl.CostEstimate(
            flops=2 * flops, bytes_accessed=32 * 1024 * 1024, transcendentals=2 * seqs * length * units
        ),
        name="block",
    )(*operands)


def finish_kernel(cfg, lens, *refs):
    terms, block, length, aliased = cfg
    parts, refs = refs[:terms], refs[terms:]
    tokens, cotangent, bias = refs[:3]
    result, grad = refs[-2:]
    at = pl.program_id(0) * block
    seq_len = lens[at // length]
    position = at % length + lax.broadcasted_iota(jnp.int32, (block, 1), 0)
    valid = position < seq_len
    total = [sum(part[...].astype(F32) for part in parts[w::2]) for w in range(2)]
    result[...] = jnp.where(valid, tokens[...].astype(F32) + total[0] + bias[0:1, :] + bias[1:2, :], 0.0)
    grad[...] = jnp.where(valid, cotangent[...].astype(F32) + total[1], 0.0)


def finish_call(chunk, lens, parts, tokens, cotangent, bias, length, earlier):
    rows, cols = tokens.shape
    span = parts[0].shape[0]
    block = min(512, length)
    base = chunk * length // block
    part_spec = pl.BlockSpec((block, cols), lambda i: (i, 0))
    row_spec = pl.BlockSpec((block, cols), lambda i: (base + i, 0))
    specs = [pl.BlockSpec(memory_space=pltpu.SMEM)] + [part_spec] * len(parts) + [row_spec] * 2
    specs += [pl.BlockSpec(bias.shape, lambda i: (0, 0))] + [pl.BlockSpec(memory_space=pl.ANY)] * len(earlier)
    operands = [lens, *parts, tokens, cotangent, bias, *earlier]
    return pl.pallas_call(
        functools.partial(finish_kernel, (len(parts), block, length, bool(earlier))),
        grid=(span // block,),
        out_shape=[jax.ShapeDtypeStruct((rows, cols), F32)] * 2,
        in_specs=specs,
        out_specs=[row_spec] * 2,
        input_output_aliases={len(operands) - 2: 0, len(operands) - 1: 1} if earlier else {},
        cost_estimate=pl.CostEstimate(flops=8 * span * cols, bytes_accessed=20 * span * cols, transcendentals=0),
        name="finish",
    )(*operands)


def merge_kernel(cfg, scal, *refs):
    sizes, dim, wide, units, rank, n_src, cut = cfg
    (w_qkv, w_up, w_down, w_out, f_split), refs = refs[:5], refs[5:]
    sources, refs = refs[:n_src], refs[n_src:]
    outs, refs = refs[:4], refs[4:]
    weights_v, outs_v, (fin_v, res0_v, res1_v, split_v, t_v, in_sems, out_sems) = refs[:4], refs[4:8], refs[8:]
    core = lax.rem(scal[0], 2)
    skip = f_split.shape[1] - split_v.shape[1]
    pairs = input_pairs(sizes, core, sources, fin_v, (res0_v, res1_v)) + [(f_split.at[:, skip:], split_v)]
    pairs += list(zip((w_qkv, w_up, w_down, w_out), weights_v))
    loads = [pltpu.make_async_copy(a, b, in_sems.at[i]) for i, (a, b) in enumerate(pairs)]
    for load in loads:
        load.start()
    for load in loads:
        load.wait()
    mixed = 3 * wide
    t_v[...] = split_v[:, mixed + units :].astype(F32).T.astype(BF)
    plans = [
        (0, dim, lambda rows: fin_v[0].reshape(dim, rank)[rows], lambda: split_v[:, :mixed]),
        (1, dim, lambda rows: fin_v[1].reshape(dim, rank)[rows], lambda: split_v[:, mixed : mixed + units]),
        (2, units, lambda rows: t_v[rows, :], lambda: res1_v[...]),
        (3, wide, lambda rows: t_v[units + rows.start : units + rows.stop, :], lambda: res0_v[...]),
    ]
    stores = []
    for which, depth, left, right in plans:
        for at in range(0, depth, cut):
            rows = slice(at, at + cut)
            outs_v[which][rows, :] = weights_v[which][rows, :].astype(F32) + mm(left(rows), right())
            copy = pltpu.make_async_copy(outs_v[which].at[rows, :], outs[which].at[rows, :], out_sems.at[len(stores)])
            copy.start()
            stores.append(copy)
    for copy in stores:
        copy.wait()


def merge_call(scal, weights, f_split, sources, sizes, dp):
    w_qkv, w_up, w_down, w_out = weights
    dim, units, wide, rank = w_up.shape[0], w_up.shape[1], w_out.shape[0], f_split.shape[0]
    high, folds, ranks, _, own_cols, direct = sizes
    cut = min(256, wide)
    ANY = pl.BlockSpec(memory_space=pl.ANY)
    chunks = (2 * dim + units + wide) // cut
    return pl.pallas_call(
        functools.partial(merge_kernel, (sizes, dim, wide, units, rank, len(sources), cut)),
        out_shape=[jax.ShapeDtypeStruct(w.shape, F32) for w in weights],
        in_specs=[pl.BlockSpec(memory_space=pltpu.SMEM)] + [ANY] * (5 + len(sources)),
        out_specs=[ANY] * 4,
        scratch_shapes=[pltpu.VMEM(w.shape, BF) for w in weights]
        + [pltpu.VMEM(w.shape, F32) for w in weights]
        + [
            pltpu.VMEM((2, dp, dim // dp, rank), BF),
            pltpu.VMEM((rank, dim), BF),
            pltpu.VMEM((rank, dim), BF),
            pltpu.VMEM((rank, 4 * wide + 2 * units), BF),
            pltpu.VMEM((units + wide, rank), BF),
            pltpu.SemaphoreType.DMA((5 + (4 * high * (folds + 1) if direct else 3),)),
            pltpu.SemaphoreType.DMA((chunks,)),
        ],
        compiler_params=pltpu.CompilerParams(vmem_limit_bytes=40 * 1024 * 1024),
        cost_estimate=pl.CostEstimate(
            flops=2 * rank * (dim * (3 * wide + 2 * units + wide)), bytes_accessed=20 * 1024 * 1024, transcendentals=0
        ),
        name="merge",
    )(scal, *weights, f_split, *sources)


def bits_of(size):
    return [1 << b for b in range(size.bit_length() - 1)]


def swap(x, axis, size, bit):
    return lax.ppermute(x, axis, [(i, i ^ bit) for i in range(size)])


def bit_value(axis, bit):
    return (lax.axis_index(axis) // bit) % 2


def halve(x, axis, size, bit):
    mine = bit_value(axis, bit)
    keep = lax.dynamic_index_in_dim(x, mine, 0, keepdims=False).astype(F32)
    give = lax.dynamic_index_in_dim(x, 1 - mine, 0, keepdims=False).astype(BF)
    return keep + swap(give, axis, size, bit).astype(F32)


def after(x, *earlier):
    return lax.optimization_barrier((x, earlier))[0]


def in_order(x, other, axis, bit):
    upper = bit_value(axis, bit) == 1
    return jnp.where(upper, other, x), jnp.where(upper, x, other)


def spread_inputs(low_in, low_res, mp, wait=()):
    own_rows, rank = low_in.shape[1:]
    own_ranks = low_res.shape[1]
    both = jnp.concatenate(
        [low_in[n, j * own_ranks : (j + 1) * own_ranks] for n in range(2) for j in range(own_rows // own_ranks)]
        + [low_res[0], low_res[1]],
        1,
    )
    if wait:
        both = after(both, *wait)
    for bit in bits_of(mp)[1:]:
        both = jnp.concatenate(in_order(both, swap(both, "mp", mp, bit), "mp", bit), 1)
    return both


def gather_rows(x, dp):
    found = lax.all_to_all(jnp.broadcast_to(x[None], (dp,) + x.shape), "dp", 0, 0, tiled=True)
    return found.reshape(dp * x.shape[0], x.shape[1])


def gather_factors(both, split, sizes, dim, dp, mp):
    high, folds, ranks, rank, own_cols, direct = sizes
    found = gather_rows(jnp.concatenate([both, split], 1), dp)
    mine = found[:, : both.shape[1]]
    other = swap(mine, "mp", mp, 1)
    if direct:
        deep = lambda x: x.reshape(dp, ranks, x.shape[1])
        return found, [deep(found), deep(other), found, other]
    cores = jnp.stack(in_order(mine, other, "mp", 1)).reshape(2, dp, ranks, high, both.shape[1] // high)
    in_part = cores[..., : 2 * folds * rank].reshape(2, dp, ranks, high, 2, folds, rank)
    res_part = cores[..., 2 * folds * rank :].reshape(2, dp, ranks, high, 2, own_cols)
    whole_in = in_part.transpose(4, 1, 3, 0, 5, 2, 6).reshape(2, dp, dim // dp, rank)
    return found, [whole_in, res_part.transpose(4, 1, 2, 3, 0, 5).reshape(2, rank, dim)]


def reduce_inputs(sums, sizes, dim, dp, mp):
    high, folds, ranks, rank, own_cols, direct = sizes
    if direct:
        in_keep, in_send, res_keep, res_send = sums
        in_both = in_keep.astype(F32) + swap(in_send, "mp", mp, 1).astype(F32)
        res_both = res_keep.astype(F32) + swap(res_send, "mp", mp, 1).astype(F32)
        both = jnp.concatenate([in_both.reshape(high, rank, -1), res_both], 2)
    else:
        in_part = sums[0].reshape(2, dp, high, 2, folds, ranks, rank)
        in_part = in_part.transpose(3, 2, 1, 5, 0, 4, 6).reshape(2, high, rank, 2 * folds * rank)
        res_part = sums[1].reshape(2, rank, high, 2, own_cols).transpose(3, 2, 1, 0, 4)
        both = halve(jnp.concatenate([in_part, res_part.reshape(2, high, rank, 2 * own_cols)], 3), "mp", mp, 1)
    both = both.reshape((2,) * len(bits_of(high)) + both.shape[1:])
    for bit in reversed(bits_of(mp)[1:]):
        both = halve(both, "mp", mp, bit)
    return both


def reduce_rows(x, dp):
    return jnp.sum(lax.all_to_all(x.reshape(dp, -1, x.shape[1]), "dp", 0, 0, tiled=True).astype(F32), 0)


def adam_step(factor, moment, gradient):
    first_moment = 0.9 * moment[0] + 0.1 * gradient
    second_moment = 0.999 * moment[1] + 0.001 * gradient * gradient
    updated = factor - 0.01 * (first_moment / first_fix) / (
        jnp.sqrt(second_moment / second_fix) + 1e-08
    )
    keep_mask = (jnp.abs(moment[0]) >= 0.5).astype(F32)
    return (updated, jnp.stack([first_moment * keep_mask, second_moment * keep_mask]))


def rope_tables(length):
    half = ROT // 2
    frequency = 10000.0 ** (-np.arange(half) * 2.0 / ROT)
    angles = np.arange(length)[:, None] * frequency[None, :]
    cos, sin = np.cos(angles), np.sin(angles)
    ones, zeros = np.ones((length, HEAD - ROT)), np.zeros((length, HEAD - ROT))
    blank = np.zeros_like(sin)
    one_head = [
        np.concatenate([cos, cos, ones], 1),
        np.concatenate([-sin, blank, zeros], 1),
        np.concatenate([blank, sin, zeros], 1),
    ]
    return jnp.asarray(np.stack([np.concatenate([t, t], 1) for t in one_head]).astype(np.float32))


def per_device(
    dp,
    mp,
    tokens,
    cotangent,
    lengths,
    norm_gain,
    norm_shift,
    qkv_weight,
    out_weight,
    up_weight,
    down_weight,
    qkv_bias,
    up_bias,
    res_bias,
    in_factor,
    qkv_factor,
    up_factor,
    out_factor,
    down_factor,
    res_factor,
    in_moments,
    qkv_moments,
    up_moments,
    out_moments,
    down_moments,
    res_moments,
):
    row_count, cols = tokens.shape
    seq_count = lengths.shape[0]
    length = row_count // seq_count
    wide = out_weight.shape[0]
    dim, units = up_weight.shape
    me = lax.axis_index("mp").astype(jnp.int32)
    mp_bits = bits_of(mp)
    plan = [(0, 2), (2, seq_count - 2)]
    chunks = len(plan)

    rank = in_factor.shape[2]
    low = lambda f: f.astype(BF)
    both = spread_inputs(low(in_factor), low(res_factor), mp)

    own_ranks, own_cols = res_factor.shape[1:]
    sizes = (mp // 2, in_factor.shape[1] // own_ranks, own_ranks, rank, own_cols, own_ranks % 16 == 0)
    rank_rows = lambda qkv, up, down, out: jnp.concatenate([low(qkv), low(up), low(down).T, low(out).T], 1)
    f_split, sources = gather_factors(
        both, rank_rows(qkv_factor, up_factor, down_factor, out_factor), sizes, dim, dp, mp
    )
    whole_rows = (tokens, cotangent, swap(tokens, "mp", mp, 1), swap(cotangent, "mp", mp, 1))

    def far_rows(c, wait):
        rows = slice(plan[c][0] * length, sum(plan[c]) * length)
        held = {0: [tokens[rows], cotangent[rows]]}
        for bit in reversed(mp_bits[1:]):
            for k in list(held):
                held[k | bit] = [swap(after(x, *wait), "mp", mp, bit) for x in held[k]]
        return {k: v for k, v in held.items() if k}

    def near_rows(held, wait):
        for k in list(held):
            held[k | 1] = [swap(after(x, *wait) if wait else x, "mp", mp, 1) for x in held[k]]
        return [x for k in sorted(held) for x in held[k]]

    small = (norm_gain, norm_shift, qkv_bias[None], up_bias[None], rope_tables(length))
    marks = [3 * wide, 3 * wide + units, 3 * wide + 2 * units]

    def pieces(packed):
        return jnp.split(packed, marks, 1)

    weights = (qkv_weight, up_weight, down_weight, out_weight)

    def near_sums(outs):
        held = {k: [outs[k], [swap(x, "mp", mp, 1) for x in outs[k | 1]]] for k in reversed(range(0, mp, 2))}
        return held, far_gives(held, mp_bits[1:2])

    def far_gives(held, bits):
        gone = [k for k in held if k & bits[0]] if bits else []
        return {k: [sum(x[w].astype(F32) for x in held[k]).astype(BF) for w in range(2)] for k in gone}

    def far_sums(held, gives, which, wait):
        terms = {k: [x[which] for x in held[k]] for k in held}
        moved = None
        for i, bit in enumerate(mp_bits[1:]):
            for k in [k for k in terms if k & bit]:
                gone = terms.pop(k)
                give = sum(x.astype(F32) for x in gone).astype(BF) if i else gives[k][which]
                moved = swap(after(give, *wait), "mp", mp, bit)
                terms[k ^ bit].append(moved)
        return terms[0], moved

    def woven(one, two):
        return [x for pair in zip(one, two) for x in pair]

    acc = None
    partials, totals = [], []
    far = far_rows(0, (both,))
    for c in range(chunks):
        begin, seqs = plan[c]
        scal = jnp.concatenate([lengths[begin : begin + seqs], me[None]])
        wait = () if c == 0 else (partials[-1][0][0],)
        received = near_rows(far, wait)
        if c + 1 < chunks:
            far = far_rows(c + 1, (received[-1],))
        if c:
            held, gives = near_sums(partials[-1])
            ended = [far_sums(held, gives, w, (received[-1],)) for w in range(2)]
            moved = [x[1] for x in ended if x[1] is not None]
            totals.append(woven(ended[0][0], ended[1][0]))
            scal = after(scal, *[x for give in gives.values() for x in give])
        found = block_call(
            begin, seqs, c == chunks - 1, sizes, acc, scal, whole_rows, received, small, weights,
            (f_split, sources), length, mp,
        )
        partials.append([found[2 * k : 2 * k + 2] for k in range(mp)])
        acc = after(found[2 * mp :], *moved) if c else found[2 * mp :]

    split_sum, *input_sums = acc
    grads_both = reduce_inputs(input_sums, sizes, dim, dp, mp)
    held, gives = near_sums(partials[-1])
    split_sum = after(split_sum, *[x for give in gives.values() for x in give])
    last_result, _ = far_sums(held, gives, 0, (grads_both,))
    owned = reduce_rows(jnp.concatenate([grads_both.astype(BF), split_sum], 1), dp)
    own_both, split_grad = owned[:, : grads_both.shape[1]], owned[:, grads_both.shape[1] :]
    cut = own_both.shape[1] - 2 * own_cols
    in_grad = own_both[:, :cut].reshape(own_ranks, 2, -1, rank).transpose(1, 2, 0, 3).reshape(in_factor.shape)
    res_grad = jnp.stack([own_both[:, cut : cut + own_cols], own_both[:, cut + own_cols :]])
    qkv_owned, up_owned, down_owned, out_owned = pieces(split_grad)
    down_owned, out_owned = down_owned.T, out_owned.T
    new_in, in_pruned = adam_step(in_factor, in_moments, in_grad)
    new_qkv, qkv_pruned = adam_step(qkv_factor, qkv_moments, qkv_owned)
    new_up, up_pruned = adam_step(up_factor, up_moments, up_owned)
    new_out, out_pruned = adam_step(out_factor, out_moments, out_owned)
    new_down, down_pruned = adam_step(down_factor, down_moments, down_owned)
    new_res, res_pruned = adam_step(res_factor, res_moments, res_grad)
    both = spread_inputs(low(new_in), low(new_res), mp, last_result[-1:])
    last_grad, _ = far_sums(held, gives, 1, (both,))
    totals.append(woven(last_result, last_grad))
    merged_qkv, merged_up, merged_down, merged_out = merge_call(
        me[None], weights,
        *gather_factors(both, rank_rows(new_qkv, new_up, new_down, new_out), sizes, dim, dp, mp), sizes, dp,
    )
    ended = []
    for c in range(chunks):
        ended = finish_call(
            plan[c][0], lengths[plan[c][0] : sum(plan[c])], totals[c], tokens, cotangent, res_bias, length, ended
        )
    result, grad_tokens = ended
    return (
        result,
        grad_tokens,
        in_grad,
        qkv_owned,
        up_owned,
        out_owned,
        down_owned,
        res_grad,
        merged_qkv,
        merged_out,
        merged_up,
        merged_down,
        in_pruned,
        qkv_pruned,
        up_pruned,
        out_pruned,
        down_pruned,
        res_pruned,
    )


def solution(mesh):
    placed = (
        P("dp", "mp"),
        P("dp", "mp"),
        P("dp"),
        P(),
        P(),
        P(None, "mp"),
        P("mp", None),
        P(None, "mp"),
        P("mp", None),
        P("mp"),
        P("mp"),
        P(None, "mp"),
        P(None, ("dp", "mp"), None),
        P("dp", "mp"),
        P("dp", "mp"),
        P("mp", "dp"),
        P("mp", "dp"),
        P(None, "dp", "mp"),
        P(None, None, ("dp", "mp"), None),
        P(None, "dp", "mp"),
        P(None, "dp", "mp"),
        P(None, "mp", "dp"),
        P(None, "mp", "dp"),
        P(None, None, "dp", "mp"),
    )
    return jax.shard_map(
        functools.partial(per_device, mesh.shape["dp"], mesh.shape["mp"]),
        mesh=mesh,
        in_specs=placed,
        out_specs=(
            P("dp", "mp"),
            P("dp", "mp"),
            P(None, ("dp", "mp"), None),
            P("dp", "mp"),
            P("dp", "mp"),
            P("mp", "dp"),
            P("mp", "dp"),
            P(None, "dp", "mp"),
            P(None, "mp"),
            P("mp", None),
            P(None, "mp"),
            P("mp", None),
            P(None, None, ("dp", "mp"), None),
            P(None, "dp", "mp"),
            P(None, "dp", "mp"),
            P(None, "mp", "dp"),
            P(None, "mp", "dp"),
            P(None, None, "dp", "mp"),
        ),
        check_vma=False,
    )
```

```python
import functools
import math

import jax
import jax.numpy as jnp
import numpy as np
from jax import lax
from jax.experimental import pallas as pl
from jax.experimental.pallas import tpu as pltpu
from jax.sharding import PartitionSpec as P

HEAD = 64
ROT = 16
BF = jnp.bfloat16
F32 = jnp.float32

first_fix = 1.0 - math.exp(100.0 * math.log(0.9))
second_fix = 1.0 - math.exp(100.0 * math.log(0.999))


def mm(a, b):
    return lax.dot_general(a, b, (((1,), (0,)), ((), ())), preferred_element_type=F32)


def mm_t(a, b):
    return lax.dot_general(a, b, (((1,), (1,)), ((), ())), preferred_element_type=F32)


def rows_mm(a, b):
    return lax.dot_general(a, b, (((0,), (0,)), ((), ())), preferred_element_type=F32)


def layer_norm(x):
    centred = x - jnp.mean(x, -1, keepdims=True)
    scale = lax.rsqrt(jnp.mean(centred * centred, -1, keepdims=True) + 1e-05)
    return centred * scale, scale


def layer_norm_back(grad_unit, unit_rows, scale):
    return scale * (
        grad_unit
        - jnp.mean(grad_unit, -1, keepdims=True)
        - unit_rows * jnp.mean(grad_unit * unit_rows, -1, keepdims=True)
    )


def rotate(values, cos, sin_a, sin_b, sign):
    width = values.shape[-1]
    turned = pltpu.roll(values, width - ROT // 2, 1) * sin_a + pltpu.roll(values, ROT // 2, 1) * sin_b
    return values * cos + turned if sign > 0 else values * cos - turned


def input_pairs(sizes, core, sources, fin_v, res_places):
    high, folds, ranks, rank, own_cols, direct = sizes
    if not direct:
        f_in, f_res = sources
        return [(f_in, fin_v), (f_res.at[0], res_places[0]), (f_res.at[1], res_places[1])]
    width = 2 * folds * rank + 2 * own_cols
    found = []
    for c in range(2):
        deep, wide2 = sources[c], sources[2 + c]
        which = core if c == 0 else 1 - core
        for y in range(high):
            for n in range(2):
                for j in range(folds):
                    at = y * width + (n * folds + j) * rank
                    rows = pl.ds(pl.multiple_of(((y * 2 + which) * folds + j) * ranks, ranks), ranks)
                    found.append((deep.at[:, :, at : at + rank], fin_v.at[n, :, rows, :]))
                at = y * width + 2 * folds * rank + n * own_cols
                place = pl.ds(pl.multiple_of((y * 2 + which) * own_cols, own_cols), own_cols)
                found.append((wide2.at[:, at : at + own_cols], res_places[n].at[:, place]))
    return found


def block_kernel(cfg, scal, *refs):
    chunk, seqs, first, last, length, tile, parts, cols, dim, wide, units, rank, sizes = cfg
    whole_rows, refs = refs[:4], refs[4:]
    received, refs = refs[: 2 * parts - 4], refs[2 * parts - 4 :]
    (gain, shift, b_qkv, b_up, rope, w_qkv, w_up, w_down), refs = refs[:8], refs[8:]
    (acc_in, res_in), refs = refs[:2], refs[2:]
    outs, refs = refs[: 2 * parts], refs[2 * parts :]
    sums, refs = refs[: len(refs) - 29], refs[len(refs) - 29 :]
    (
        gin_b, gres_b, gsplit_b, x_v, c_v, wq_v, wu_v, wd_v, rope_v, acc_v, res_v,
        q_s, k_s, v_s, g_s, qt_s, gt_s, gq_s, gkt_s, gvt_s, ac_s, p_s, qr_s, gor_s, out_v,
        row_sems, w_sems, out_sems, acc_sems,
    ) = refs
    me = scal[seqs]
    core = lax.rem(me, 2)
    steps = length // tile
    mixed_cols = 3 * wide
    joint = units + wide

    def tiles_of(s):
        return (scal[s] + tile - 1) // tile

    def row_slice(t, size=tile):
        return pl.ds(pl.multiple_of(t * tile, tile), size)


    def row_copies(s, t):
        found = []
        slot = lax.rem(s, 2)
        for which, dest in enumerate((x_v, c_v)):
            for k in range(parts):
                at = pl.ds(pl.multiple_of(s * length + t * tile, tile), tile)
                if k < 2:
                    src = whole_rows[2 * k + which].at[
                        pl.ds(pl.multiple_of((chunk + s) * length + t * tile, tile), tile), :
                    ]
                else:
                    src = received[2 * (k - 2) + which].at[at, :]
                place = pl.ds(pl.multiple_of(jnp.bitwise_xor(me, k) * cols, cols), cols)
                found.append(
                    pltpu.make_async_copy(
                        src, dest.at[slot, row_slice(t), place], row_sems.at[slot, t, which * parts + k]
                    )
                )
        return found

    def start_rows(s):
        def one(t, carry):
            for copy in row_copies(s, t):
                copy.start()
            return carry

        lax.fori_loop(0, tiles_of(s), one, 0)

    def out_copies(s, t):
        found = []
        for which in range(2):
            for k in range(parts):
                place = pl.ds(pl.multiple_of(jnp.bitwise_xor(me, k) * cols, cols), cols)
                rows = pl.ds(pl.multiple_of(s * length + t * tile, tile), tile)
                found.append(
                    pltpu.make_async_copy(
                        out_v.at[which, row_slice(t), place],
                        outs[2 * k + which].at[rows, :],
                        out_sems.at[t, which * parts + k],
                    )
                )
        return found

    def drain(s):
        def one(t, carry):
            for copy in out_copies(s, t):
                copy.wait()
            return carry

        lax.fori_loop(0, tiles_of(s), one, 0)

    pairs = [(w_up, wu_v), (w_down, wd_v), (w_qkv, wq_v), (rope, rope_v)]
    loads = [pltpu.make_async_copy(a, b, w_sems.at[i]) for i, (a, b) in enumerate(pairs)]
    start_rows(0)
    for load in loads:
        load.start()
    back_in = []
    if first:
        acc_v[...] = jnp.zeros_like(acc_v)
        res_v[...] = jnp.zeros_like(res_v)
    else:
        back_in = [
            pltpu.make_async_copy(acc_in, acc_v, acc_sems.at[0]),
            pltpu.make_async_copy(res_in, res_v, acc_sems.at[1]),
        ]
        for copy in back_in:
            copy.start()
    for load in loads:
        load.wait()
    for copy in back_in:
        copy.wait()
    c_in0, c_in1, c_qkv, c_up, c_down, c_out = (
        slice(0, dim),
        slice(dim, 2 * dim),
        slice(2 * dim, 2 * dim + mixed_cols),
        slice(2 * dim + mixed_cols, 2 * dim + mixed_cols + units),
        slice(2 * dim + mixed_cols + units, 2 * dim + mixed_cols + 2 * units),
        slice(2 * dim + mixed_cols + 2 * units, 2 * dim + mixed_cols + 2 * units + wide),
    )
    lane = lax.broadcasted_iota(jnp.int32, (1, 128), 1)
    left = lane < HEAD

    def one_sequence(s, carry):
        seq_len = scal[s]
        count = tiles_of(s)
        slot = lax.rem(s, 2)

        @pl.when(s + 1 < seqs)
        def _():
            start_rows(s + 1)

        gkt_s[...] = jnp.zeros_like(gkt_s)
        gvt_s[...] = jnp.zeros_like(gvt_s)

        def upstream(t, size):
            position = t * tile + lax.broadcasted_iota(jnp.int32, (size, 1), 0)
            return jnp.where(position < seq_len, c_v[slot, row_slice(t, size), :].astype(F32), 0.0).astype(BF)

        def tables(t, size):
            rows = row_slice(t, size)
            return [jnp.concatenate([rope_v[i, rows, :]] * (wide // 128), 1) for i in range(3)]

        def forward(t, size):
            rows = row_slice(t, size)
            for j in range(size // tile):
                for copy in row_copies(s, t + j):
                    copy.wait()
            unit, _ = layer_norm(x_v[slot, rows, :].astype(F32))
            low_one = (unit * gain[0:1, :] + shift[0:1, :]).astype(BF)
            low_two = (unit * gain[1:2, :] + shift[1:2, :]).astype(BF)
            ups = upstream(t, size)
            hidden = mm(low_two, wu_v[:dim, :])
            back = mm_t(ups, wd_v[:, :dim])
            mixed = mm(low_one, wq_v[:dim, :])
            code_up = hidden[:, units:]
            hidden = hidden[:, :units] + b_up[...]
            code_qkv = mixed[:, mixed_cols:]
            mixed = mixed[:, :mixed_cols] + mm(code_qkv.astype(BF), wq_v[dim:, :mixed_cols]) + b_qkv[...]
            blocks = [mixed[:, i * 128 : (i + 1) * 128] for i in range(mixed_cols // 128)]
            cat = lambda found: jnp.concatenate(found, 1) if len(found) > 1 else found[0]
            q_mixed = cat([jnp.where(left, blocks[3 * p], blocks[3 * p + 1]) for p in range(wide // 128)])
            k_mixed = cat(
                [pltpu.roll(jnp.where(left, blocks[3 * p + 2], blocks[3 * p]), HEAD, 1) for p in range(wide // 128)]
            )
            v_mixed = cat([jnp.where(left, blocks[3 * p + 1], blocks[3 * p + 2]) for p in range(wide // 128)])
            cdf = 0.5 * (1.0 + lax.erf(hidden * (1.0 / math.sqrt(2.0))))
            active = (hidden * cdf).astype(BF)
            slope = cdf + hidden * (jnp.exp(-0.5 * hidden * hidden) * (1.0 / math.sqrt(2.0 * math.pi)))
            grad_hidden = (back[:, :units] * slope).astype(BF)
            ac_s[rows, :units] = active
            cos, sin_a, sin_b = tables(t, size)
            query = rotate(q_mixed, cos, sin_a, sin_b, 1).astype(BF).astype(F32) * HEAD**-0.5
            q_s[rows, :] = query.astype(BF)
            qt_s[:, rows] = query.T.astype(BF)
            k_s[rows, :] = rotate(k_mixed, cos, sin_a, sin_b, 1).astype(BF)
            v_s[rows, :] = v_mixed.astype(BF)
            qr_s[:, rows] = code_qkv.T.astype(BF)
            grad_context = back[:, units:joint]
            g_s[rows, :] = grad_context.astype(BF)
            gt_s[:, rows] = grad_context.T.astype(BF)
            gor_s[:, rows] = back[:, joint + rank :].T.astype(BF)
            below = mm_t(grad_hidden, wu_v[:, :units])
            p_s[rows, :] = below[:, :dim] * gain[1:2, :]
            acc_v[:, c_up] += mm(code_up.T.astype(BF), grad_hidden)
            acc_v[:, c_down] += mm(back[:, joint : joint + rank].T.astype(BF), active)
            acc_v[:, c_in1] += mm(below[:, dim:].T.astype(BF), low_two)

        def finish(t, size):
            rows = row_slice(t, size)
            cos, sin_a, sin_b = tables(t, size)
            grad_q = rotate(gq_s[rows, :], cos, sin_a, sin_b, -1)
            grad_k = rotate(gkt_s[:, rows].T, cos, sin_a, sin_b, -1)
            grad_v = gvt_s[:, rows].T
            blocks = []
            for p in range(wide // 128):
                pair = slice(p * 128, (p + 1) * 128)
                one_q, one_k, one_v = grad_q[:, pair], pltpu.roll(grad_k[:, pair], HEAD, 1), grad_v[:, pair]
                blocks += [jnp.where(left, one_q, one_k), jnp.where(left, one_v, one_q), jnp.where(left, one_k, one_v)]
            grad_mixed = jnp.concatenate(blocks, 1).astype(BF)
            below = mm_t(grad_mixed, wq_v[:, :mixed_cols])
            both = ac_s[rows, :]
            ahead = mm(both, wd_v[:joint, :])
            unit, scale = layer_norm(x_v[slot, rows, :].astype(F32))
            low_one = (unit * gain[0:1, :] + shift[0:1, :]).astype(BF)
            out_v[0, rows, :] = ahead[:, :dim].astype(BF)
            grad_code = below[:, dim:]
            grad_norm = below[:, :dim] + mm_t(grad_code.astype(BF), wq_v[:dim, mixed_cols:])
            grad_unit = grad_norm * gain[0:1, :] + p_s[rows, :]
            out_v[1, rows, :] = layer_norm_back(grad_unit, unit, scale).astype(BF)
            for j in range(size // tile):
                for copy in out_copies(s, t + j):
                    copy.start()
            acc_v[:, c_in0] += mm(grad_code.T.astype(BF), low_one)
            acc_v[:, c_qkv] += mm(qr_s[:, rows], grad_mixed)
            acc_v[:, c_out] += mm(gor_s[:, rows], both[:, units:])
            res_v[...] += mm(ahead[:, dim:].T.astype(BF), upstream(t, size))

        def over_rows(work):
            def single(j, carry):
                work(j, tile)
                return carry

            lax.fori_loop(0, count, single, 0)

        over_rows(forward)

        for i in range(steps):
            @pl.when(i < count)
            def _(i=i):
                qrows = pl.ds(i * tile, tile)
                before, extent = i * tile, (i + 1) * tile
                qpos = before + lax.broadcasted_iota(jnp.int32, (tile, tile), 0)
                kpos = before + lax.broadcasted_iota(jnp.int32, (tile, tile), 1)
                allowed = (kpos <= qpos) & (kpos < seq_len)
                allowed = jnp.concatenate([allowed, allowed], 0)
                def one_pair(p, carry):
                    pair = pl.ds(pl.multiple_of(p * 128, 128), 128)
                    q_all, g_all = q_s[qrows, pair], g_s[qrows, pair]
                    zero = jnp.zeros_like(q_all)
                    q_two = jnp.concatenate([jnp.where(left, q_all, zero), jnp.where(left, zero, q_all)], 0)
                    g_two = jnp.concatenate([jnp.where(left, g_all, zero), jnp.where(left, zero, g_all)], 0)
                    keys, vals = k_s[:extent, pair], v_s[:extent, pair]
                    scores = mm_t(q_two, keys)
                    grad_probs = mm_t(g_two, vals)
                    last = jnp.where(allowed, scores[:, before:], -1e30)
                    scores = jnp.concatenate([scores[:, :before], last], 1) if i else last
                    weights = jnp.exp(scores - jnp.max(scores, -1, keepdims=True))
                    probs = weights * (1.0 / jnp.sum(weights, -1, keepdims=True))
                    low_probs = probs.astype(BF)
                    context = mm(low_probs, vals)
                    row_term = jnp.sum(probs * grad_probs, -1, keepdims=True)
                    grad_scores = (probs * (grad_probs - row_term)).astype(BF)
                    grad_q = mm(grad_scores, keys)
                    ac_s[qrows, pl.ds(pl.multiple_of(units + p * 128, 128), 128)] = jnp.where(
                        left, context[:tile], context[tile:]
                    ).astype(BF)
                    gq_s[qrows, pair] = jnp.where(left, grad_q[:tile], grad_q[tile:]) * HEAD**-0.5
                    for h in range(2):
                        feats = pl.ds(pl.multiple_of(p * 128 + h * HEAD, HEAD), HEAD)
                        part = slice(h * tile, (h + 1) * tile)
                        gkt_s[feats, :extent] += mm(qt_s[feats, qrows], grad_scores[part])
                        gvt_s[feats, :extent] += mm(gt_s[feats, qrows], low_probs[part])
                    return carry

                lax.fori_loop(0, wide // 128, one_pair, 0)

        @pl.when(s > 0)
        def _():
            drain(s - 1)

        over_rows(finish)
        return carry

    lax.fori_loop(0, seqs, one_sequence, 0)
    if not last:
        targets = [(acc_v, sums[0]), (res_v, sums[1])]
    else:
        high, folds, ranks, _, own_cols, direct = sizes
        gsplit_b[...] = acc_v[:, 2 * dim :].astype(BF)
        gres_b[:rank, :] = res_v[rank:, :].astype(BF)
        gres_b[rank:, :] = res_v[:rank, :].astype(BF)
        for n, place in enumerate((c_in0, c_in1)):
            gin_b[n] = acc_v[:, place].T.astype(BF).reshape(gin_b.shape[1:])
        targets = [(gsplit_b, sums[0])]
        if not direct:
            targets += [(gin_b, sums[1]), (gres_b, sums[2])]
        else:
            for c in range(2):
                which = core if c == 0 else 1 - core
                for y in range(high):
                    for n in range(2):
                        for j in range(folds):
                            at = (n * folds + j) * rank
                            rows = pl.ds(pl.multiple_of(((y * 2 + which) * folds + j) * ranks, ranks), ranks)
                            targets.append((gin_b.at[n, :, rows, :], sums[1 + c].at[y, :, :, at : at + rank]))
                        place = pl.ds(pl.multiple_of((y * 2 + which) * own_cols, own_cols), own_cols)
                        targets.append(
                            (gres_b.at[n * rank : (n + 1) * rank, place],
                             sums[3 + c].at[y, :, n * own_cols : (n + 1) * own_cols])
                        )
    back_out = [pltpu.make_async_copy(a, b, acc_sems.at[2 + i]) for i, (a, b) in enumerate(targets)]
    for copy in back_out:
        copy.start()
    drain(seqs - 1)
    for copy in back_out:
        copy.wait()


def prepare_kernel(cfg, scal, *refs):
    sizes, dim, wide, units, rank, n_src = cfg
    (w_qkv, w_up, w_down, w_out, f_split), refs = refs[:5], refs[5:]
    sources, refs = refs[:n_src], refs[n_src:]
    outs, (wq_v, wu_v, wd_v, ft_v, fin_v, w_sems, out_sems) = refs[:3], refs[3:]
    core = lax.rem(scal[0], 2)
    mixed_cols = 3 * wide
    joint = units + wide
    skip = f_split.shape[1] - mixed_cols - units - joint
    res_places = (wd_v.at[joint + rank :, :dim], wd_v.at[joint : joint + rank, :dim])
    pairs = [
        (w_qkv, wq_v.at[:dim, :mixed_cols]),
        (f_split.at[:, skip : skip + mixed_cols], wq_v.at[dim:, :mixed_cols]),
        (w_up, wu_v.at[:dim, :units]),
        (f_split.at[:, skip + mixed_cols : skip + mixed_cols + units], wu_v.at[dim:, :units]),
        (w_down, wd_v.at[:units, :dim]),
        (w_out, wd_v.at[units:joint, :dim]),
        (f_split.at[:, skip + mixed_cols + units :], ft_v),
    ] + input_pairs(sizes, core, sources, fin_v, res_places)
    loads = [pltpu.make_async_copy(a, b, w_sems.at[i]) for i, (a, b) in enumerate(pairs)]
    for load in loads:
        load.start()
    wd_v[:units, dim + rank :] = jnp.zeros((units, rank), BF)
    wd_v[units:joint, dim : dim + rank] = jnp.zeros((wide, rank), BF)
    wq_v[dim:, mixed_cols:] = jnp.zeros((rank, rank), BF)
    wu_v[dim:, units:] = jnp.zeros((rank, rank), BF)
    wd_v[joint:, dim:] = jnp.zeros((2 * rank, 2 * rank), BF)
    for load in loads:
        load.wait()
    wd_v[:units, dim : dim + rank] = ft_v[:, :units].astype(F32).T.astype(BF)
    wd_v[units:joint, dim + rank :] = ft_v[:, units:].astype(F32).T.astype(BF)
    wq_v[:dim, mixed_cols:] = fin_v[0].reshape(dim, rank)
    wu_v[:dim, units:] = fin_v[1].reshape(dim, rank)

    def whole(ref, top, depth, width, cut, other, at):
        def one(i, carry):
            rows = pl.ds(pl.multiple_of(top + i * cut, cut), cut)
            low_rank = mm(ref[rows, at : at + rank], other())
            ref[rows, :width] = (ref[rows, :width].astype(F32) + low_rank).astype(BF)
            return carry

        lax.fori_loop(0, depth // cut, one, 0)

    cut = min(256, units, wide)
    whole(wu_v, 0, dim, units, cut, lambda: wu_v[dim:, :units], units)
    whole(wd_v, 0, units, dim, cut, lambda: wd_v[joint : joint + rank, :dim], dim)
    whole(wd_v, units, wide, dim, cut, lambda: wd_v[joint + rank :, :dim], dim + rank)
    stores = [pltpu.make_async_copy(a, b, out_sems.at[i]) for i, (a, b) in enumerate(zip((wq_v, wu_v, wd_v), outs))]
    for store in stores:
        store.start()
    for store in stores:
        store.wait()


def prepare_call(scal, weights, f_split, sources, sizes, dp):
    w_qkv, w_up, w_down, w_out = weights
    dim, units, wide, rank = w_up.shape[0], w_up.shape[1], w_out.shape[0], f_split.shape[0]
    high, folds, ranks, _, own_cols, direct = sizes
    ANY = pl.BlockSpec(memory_space=pl.ANY)
    shapes = [(dim + rank, 3 * wide + rank), (dim + rank, units + rank), (units + wide + 2 * rank, dim + 2 * rank)]
    return pl.pallas_call(
        functools.partial(prepare_kernel, (sizes, dim, wide, units, rank, len(sources))),
        out_shape=[jax.ShapeDtypeStruct(shape, BF) for shape in shapes],
        in_specs=[pl.BlockSpec(memory_space=pltpu.SMEM)] + [ANY] * (5 + len(sources)),
        out_specs=[ANY] * 3,
        scratch_shapes=[pltpu.VMEM(shape, BF) for shape in shapes]
        + [
            pltpu.VMEM((rank, units + wide), BF),
            pltpu.VMEM((2, dp, dim // dp, rank), BF),
            pltpu.SemaphoreType.DMA((7 + (4 * high * (folds + 1) if direct else 3),)),
            pltpu.SemaphoreType.DMA((3,)),
        ],
        compiler_params=pltpu.CompilerParams(vmem_limit_bytes=60 * 1024 * 1024),
        cost_estimate=pl.CostEstimate(
            flops=2 * rank * dim * (2 * units + wide), bytes_accessed=16 * 1024 * 1024, transcendentals=0
        ),
        name="prepare",
    )(scal, *weights, f_split, *sources)


def block_call(chunk, seqs, last, sizes, acc, scal, whole_rows, received, small, weights, length, parts):
    gain, shift, b_qkv, b_up, rope = small
    high, folds, ranks, rank, own_cols, direct = sizes
    dim, units = weights[1].shape[0] - rank, weights[1].shape[1] - rank
    wide = weights[2].shape[0] - 2 * rank - units
    dp = rank // ranks
    cols = dim // parts
    tile = 256 if length % 256 == 0 else 128
    steps = length // tile
    first = acc is None
    acc_shape = jax.ShapeDtypeStruct((rank, 2 * dim + 4 * wide + 2 * units), F32)
    res_shape = jax.ShapeDtypeStruct((2 * rank, dim), F32)
    if first:
        acc = (jnp.zeros((8, 128), F32), jnp.zeros((8, 128), F32))
    cfg = (chunk, seqs, first, last, length, tile, parts, cols, dim, wide, units, rank, sizes)
    ANY = pl.BlockSpec(memory_space=pl.ANY)
    VM = pl.BlockSpec(memory_space=pltpu.VMEM)
    operands = [scal, *whole_rows, *received, gain, shift, b_qkv, b_up, rope, *weights, *acc]
    specs = [pl.BlockSpec(memory_space=pltpu.SMEM)] + [ANY] * (2 * parts) + [VM] * 4 + [ANY] * 6
    flops = 2 * seqs * length * (dim * (units * 4 + wide * 8 + rank * 12) + units * rank * 6 + length * wide * 12)
    out = [jax.ShapeDtypeStruct((seqs * length, cols), BF)] * (2 * parts)
    if not last:
        sums = [acc_shape, res_shape]
    else:
        sums = [jax.ShapeDtypeStruct((rank, 4 * wide + 2 * units), BF)]
        if direct:
            sums += [jax.ShapeDtypeStruct((high, dp, ranks, 2 * folds * rank), BF)] * 2
            sums += [jax.ShapeDtypeStruct((high, rank, 2 * own_cols), BF)] * 2
        else:
            sums += [jax.ShapeDtypeStruct((2, dp, dim // dp, rank), BF), jax.ShapeDtypeStruct((2 * rank, dim), BF)]
    in_shape = (2, dp, dim // dp, rank)
    tall = lambda n, dtype: pltpu.VMEM((length, n), dtype)
    flat = lambda n, dtype: pltpu.VMEM((n, length), dtype)
    return pl.pallas_call(
        functools.partial(block_kernel, cfg),
        out_shape=[*out, *sums],
        in_specs=specs,
        out_specs=[ANY] * (2 * parts + len(sums)),
        scratch_shapes=[
            pltpu.VMEM(in_shape if last else (2, 1, 16, rank), BF),
            pltpu.VMEM((2 * rank, dim) if last else (16, 128), BF),
            pltpu.VMEM((rank, 4 * wide + 2 * units) if last else (16, 128), BF),
            pltpu.VMEM((2, length, dim), BF),
            pltpu.VMEM((2, length, dim), BF),
            pltpu.VMEM((dim + rank, 3 * wide + rank), BF),
            pltpu.VMEM((dim + rank, units + rank), BF),
            pltpu.VMEM((units + wide + 2 * rank, dim + 2 * rank), BF),
            pltpu.VMEM(rope.shape, F32),
            pltpu.VMEM(acc_shape.shape, F32),
            pltpu.VMEM(res_shape.shape, F32),
            tall(wide, BF), tall(wide, BF), tall(wide, BF), tall(wide, BF),
            flat(wide, BF), flat(wide, BF),
            tall(wide, F32), flat(wide, F32), flat(wide, F32),
            tall(units + wide, BF), tall(dim, F32),
            flat(rank, BF), flat(rank, BF),
            pltpu.VMEM((2, length, dim), BF),
            pltpu.SemaphoreType.DMA((2, steps, 2 * parts)),
            pltpu.SemaphoreType.DMA((4,)),
            pltpu.SemaphoreType.DMA((steps, 2 * parts)),
            pltpu.SemaphoreType.DMA((5 + 4 * high * (folds + 1),)),
        ],
        input_output_aliases={} if first or last else {len(operands) - 2: 2 * parts, len(operands) - 1: 2 * parts + 1},
        compiler_params=pltpu.CompilerParams(vmem_limit_bytes=60 * 1024 * 1024),
        cost_estimate=pl.CostEstimate(
            flops=2 * flops, bytes_accessed=32 * 1024 * 1024, transcendentals=2 * seqs * length * units
        ),
        name="block",
    )(*operands)


def finish_kernel(cfg, lens, *refs):
    terms, block, length, aliased = cfg
    parts, refs = refs[:terms], refs[terms:]
    tokens, cotangent, bias = refs[:3]
    result, grad = refs[-2:]
    at = pl.program_id(0) * block
    seq_len = lens[at // length]
    position = at % length + lax.broadcasted_iota(jnp.int32, (block, 1), 0)
    valid = position < seq_len
    total = [sum(part[...].astype(F32) for part in parts[w::2]) for w in range(2)]
    result[...] = jnp.where(valid, tokens[...].astype(F32) + total[0] + bias[0:1, :] + bias[1:2, :], 0.0)
    grad[...] = jnp.where(valid, cotangent[...].astype(F32) + total[1], 0.0)


def finish_call(chunk, lens, parts, tokens, cotangent, bias, length, earlier):
    rows, cols = tokens.shape
    span = parts[0].shape[0]
    block = min(512, length)
    base = chunk * length // block
    part_spec = pl.BlockSpec((block, cols), lambda i: (i, 0))
    row_spec = pl.BlockSpec((block, cols), lambda i: (base + i, 0))
    specs = [pl.BlockSpec(memory_space=pltpu.SMEM)] + [part_spec] * len(parts) + [row_spec] * 2
    specs += [pl.BlockSpec(bias.shape, lambda i: (0, 0))] + [pl.BlockSpec(memory_space=pl.ANY)] * len(earlier)
    operands = [lens, *parts, tokens, cotangent, bias, *earlier]
    return pl.pallas_call(
        functools.partial(finish_kernel, (len(parts), block, length, bool(earlier))),
        grid=(span // block,),
        out_shape=[jax.ShapeDtypeStruct((rows, cols), F32)] * 2,
        in_specs=specs,
        out_specs=[row_spec] * 2,
        input_output_aliases={len(operands) - 2: 0, len(operands) - 1: 1} if earlier else {},
        cost_estimate=pl.CostEstimate(flops=8 * span * cols, bytes_accessed=20 * span * cols, transcendentals=0),
        name="finish",
    )(*operands)


def merge_kernel(cfg, scal, *refs):
    sizes, dim, wide, units, rank, n_src, cut = cfg
    (w_qkv, w_up, w_down, w_out, f_split), refs = refs[:5], refs[5:]
    sources, refs = refs[:n_src], refs[n_src:]
    outs, refs = refs[:4], refs[4:]
    weights_v, outs_v, (fin_v, res0_v, res1_v, split_v, t_v, in_sems, out_sems) = refs[:4], refs[4:8], refs[8:]
    core = lax.rem(scal[0], 2)
    skip = f_split.shape[1] - split_v.shape[1]
    pairs = input_pairs(sizes, core, sources, fin_v, (res0_v, res1_v)) + [(f_split.at[:, skip:], split_v)]
    pairs += list(zip((w_qkv, w_up, w_down, w_out), weights_v))
    loads = [pltpu.make_async_copy(a, b, in_sems.at[i]) for i, (a, b) in enumerate(pairs)]
    for load in loads:
        load.start()
    for load in loads:
        load.wait()
    mixed = 3 * wide
    t_v[...] = split_v[:, mixed + units :].astype(F32).T.astype(BF)
    plans = [
        (0, dim, lambda rows: fin_v[0].reshape(dim, rank)[rows], lambda: split_v[:, :mixed]),
        (1, dim, lambda rows: fin_v[1].reshape(dim, rank)[rows], lambda: split_v[:, mixed : mixed + units]),
        (2, units, lambda rows: t_v[rows, :], lambda: res1_v[...]),
        (3, wide, lambda rows: t_v[units + rows.start : units + rows.stop, :], lambda: res0_v[...]),
    ]
    stores = []
    for which, depth, left, right in plans:
        for at in range(0, depth, cut):
            rows = slice(at, at + cut)
            outs_v[which][rows, :] = weights_v[which][rows, :].astype(F32) + mm(left(rows), right())
            copy = pltpu.make_async_copy(outs_v[which].at[rows, :], outs[which].at[rows, :], out_sems.at[len(stores)])
            copy.start()
            stores.append(copy)
    for copy in stores:
        copy.wait()


def merge_call(scal, weights, f_split, sources, sizes, dp):
    w_qkv, w_up, w_down, w_out = weights
    dim, units, wide, rank = w_up.shape[0], w_up.shape[1], w_out.shape[0], f_split.shape[0]
    high, folds, ranks, _, own_cols, direct = sizes
    cut = min(256, wide)
    ANY = pl.BlockSpec(memory_space=pl.ANY)
    chunks = (2 * dim + units + wide) // cut
    return pl.pallas_call(
        functools.partial(merge_kernel, (sizes, dim, wide, units, rank, len(sources), cut)),
        out_shape=[jax.ShapeDtypeStruct(w.shape, F32) for w in weights],
        in_specs=[pl.BlockSpec(memory_space=pltpu.SMEM)] + [ANY] * (5 + len(sources)),
        out_specs=[ANY] * 4,
        scratch_shapes=[pltpu.VMEM(w.shape, BF) for w in weights]
        + [pltpu.VMEM(w.shape, F32) for w in weights]
        + [
            pltpu.VMEM((2, dp, dim // dp, rank), BF),
            pltpu.VMEM((rank, dim), BF),
            pltpu.VMEM((rank, dim), BF),
            pltpu.VMEM((rank, 4 * wide + 2 * units), BF),
            pltpu.VMEM((units + wide, rank), BF),
            pltpu.SemaphoreType.DMA((5 + (4 * high * (folds + 1) if direct else 3),)),
            pltpu.SemaphoreType.DMA((chunks,)),
        ],
        compiler_params=pltpu.CompilerParams(vmem_limit_bytes=60 * 1024 * 1024),
        cost_estimate=pl.CostEstimate(
            flops=2 * rank * (dim * (3 * wide + 2 * units + wide)), bytes_accessed=20 * 1024 * 1024, transcendentals=0
        ),
        name="merge",
    )(scal, *weights, f_split, *sources)


def bits_of(size):
    return [1 << b for b in range(size.bit_length() - 1)]


def swap(x, axis, size, bit):
    return lax.ppermute(x, axis, [(i, i ^ bit) for i in range(size)])


def bit_value(axis, bit):
    return (lax.axis_index(axis) // bit) % 2


def halve(x, axis, size, bit):
    mine = bit_value(axis, bit)
    keep = lax.dynamic_index_in_dim(x, mine, 0, keepdims=False).astype(F32)
    give = lax.dynamic_index_in_dim(x, 1 - mine, 0, keepdims=False).astype(BF)
    return keep + swap(give, axis, size, bit).astype(F32)


def after(x, *earlier):
    return lax.optimization_barrier((x, earlier))[0]


def in_order(x, other, axis, bit):
    upper = bit_value(axis, bit) == 1
    return jnp.where(upper, other, x), jnp.where(upper, x, other)


def spread_inputs(low_in, low_res, mp, wait=()):
    own_rows, rank = low_in.shape[1:]
    own_ranks = low_res.shape[1]
    both = jnp.concatenate(
        [low_in[n, j * own_ranks : (j + 1) * own_ranks] for n in range(2) for j in range(own_rows // own_ranks)]
        + [low_res[0], low_res[1]],
        1,
    )
    if wait:
        both = after(both, *wait)
    for bit in bits_of(mp)[1:]:
        both = jnp.concatenate(in_order(both, swap(both, "mp", mp, bit), "mp", bit), 1)
    return both


def gather_rows(x, dp):
    found = lax.all_to_all(jnp.broadcast_to(x[None], (dp,) + x.shape), "dp", 0, 0, tiled=True)
    return found.reshape(dp * x.shape[0], x.shape[1])


def gather_factors(both, split, sizes, dim, dp, mp):
    high, folds, ranks, rank, own_cols, direct = sizes
    found = gather_rows(jnp.concatenate([both, split], 1), dp)
    mine = found[:, : both.shape[1]]
    other = swap(mine, "mp", mp, 1)
    if direct:
        deep = lambda x: x.reshape(dp, ranks, x.shape[1])
        return found, [deep(found), deep(other), found, other]
    cores = jnp.stack(in_order(mine, other, "mp", 1)).reshape(2, dp, ranks, high, both.shape[1] // high)
    in_part = cores[..., : 2 * folds * rank].reshape(2, dp, ranks, high, 2, folds, rank)
    res_part = cores[..., 2 * folds * rank :].reshape(2, dp, ranks, high, 2, own_cols)
    whole_in = in_part.transpose(4, 1, 3, 0, 5, 2, 6).reshape(2, dp, dim // dp, rank)
    return found, [whole_in, res_part.transpose(4, 1, 2, 3, 0, 5).reshape(2, rank, dim)]


def reduce_inputs(sums, sizes, dim, dp, mp):
    high, folds, ranks, rank, own_cols, direct = sizes
    if direct:
        in_keep, in_send, res_keep, res_send = sums
        in_both = in_keep.astype(F32) + swap(in_send, "mp", mp, 1).astype(F32)
        res_both = res_keep.astype(F32) + swap(res_send, "mp", mp, 1).astype(F32)
        both = jnp.concatenate([in_both.reshape(high, rank, -1), res_both], 2)
    else:
        in_part = sums[0].reshape(2, dp, high, 2, folds, ranks, rank)
        in_part = in_part.transpose(3, 2, 1, 5, 0, 4, 6).reshape(2, high, rank, 2 * folds * rank)
        res_part = sums[1].reshape(2, rank, high, 2, own_cols).transpose(3, 2, 1, 0, 4)
        both = halve(jnp.concatenate([in_part, res_part.reshape(2, high, rank, 2 * own_cols)], 3), "mp", mp, 1)
    both = both.reshape((2,) * len(bits_of(high)) + both.shape[1:])
    for bit in reversed(bits_of(mp)[1:]):
        both = halve(both, "mp", mp, bit)
    return both


def reduce_rows(x, dp):
    return jnp.sum(lax.all_to_all(x.reshape(dp, -1, x.shape[1]), "dp", 0, 0, tiled=True).astype(F32), 0)


def adam_step(factor, moment, gradient):
    first_moment = 0.9 * moment[0] + 0.1 * gradient
    second_moment = 0.999 * moment[1] + 0.001 * gradient * gradient
    updated = factor - 0.01 * (first_moment / first_fix) / (
        jnp.sqrt(second_moment / second_fix) + 1e-08
    )
    keep_mask = (jnp.abs(moment[0]) >= 0.5).astype(F32)
    return (updated, jnp.stack([first_moment * keep_mask, second_moment * keep_mask]))


def rope_tables(length):
    half = ROT // 2
    frequency = 10000.0 ** (-np.arange(half) * 2.0 / ROT)
    angles = np.arange(length)[:, None] * frequency[None, :]
    cos, sin = np.cos(angles), np.sin(angles)
    ones, zeros = np.ones((length, HEAD - ROT)), np.zeros((length, HEAD - ROT))
    blank = np.zeros_like(sin)
    one_head = [
        np.concatenate([cos, cos, ones], 1),
        np.concatenate([-sin, blank, zeros], 1),
        np.concatenate([blank, sin, zeros], 1),
    ]
    return jnp.asarray(np.stack([np.concatenate([t, t], 1) for t in one_head]).astype(np.float32))


def per_device(
    dp,
    mp,
    tokens,
    cotangent,
    lengths,
    norm_gain,
    norm_shift,
    qkv_weight,
    out_weight,
    up_weight,
    down_weight,
    qkv_bias,
    up_bias,
    res_bias,
    in_factor,
    qkv_factor,
    up_factor,
    out_factor,
    down_factor,
    res_factor,
    in_moments,
    qkv_moments,
    up_moments,
    out_moments,
    down_moments,
    res_moments,
):
    row_count, cols = tokens.shape
    seq_count = lengths.shape[0]
    length = row_count // seq_count
    wide = out_weight.shape[0]
    dim, units = up_weight.shape
    me = lax.axis_index("mp").astype(jnp.int32)
    mp_bits = bits_of(mp)
    plan = [(0, 2), (2, seq_count - 2)]
    chunks = len(plan)

    rank = in_factor.shape[2]
    low = lambda f: f.astype(BF)
    both = spread_inputs(low(in_factor), low(res_factor), mp)

    own_ranks, own_cols = res_factor.shape[1:]
    sizes = (mp // 2, in_factor.shape[1] // own_ranks, own_ranks, rank, own_cols, own_ranks % 16 == 0)
    rank_rows = lambda qkv, up, down, out: jnp.concatenate([low(qkv), low(up), low(down).T, low(out).T], 1)
    first_rows = [after(x[: plan[0][1] * length], both) for x in (tokens, cotangent)]
    f_split, sources = gather_factors(
        after(both, *first_rows), rank_rows(qkv_factor, up_factor, down_factor, out_factor), sizes, dim, dp, mp
    )
    whole_rows = (tokens, cotangent, swap(tokens, "mp", mp, 1), swap(cotangent, "mp", mp, 1))

    def far_rows(c, wait):
        rows = slice(plan[c][0] * length, sum(plan[c]) * length)
        held = {0: first_rows if c == 0 else [tokens[rows], cotangent[rows]]}
        for bit in reversed(mp_bits[1:]):
            for k in list(held):
                held[k | bit] = [swap(after(x, *wait), "mp", mp, bit) for x in held[k]]
        return {k: v for k, v in held.items() if k}

    def near_rows(held, wait):
        for k in list(held):
            held[k | 1] = [swap(after(x, *wait) if wait else x, "mp", mp, 1) for x in held[k]]
        return [x for k in sorted(held) for x in held[k]]

    small = (norm_gain, norm_shift, qkv_bias[None], up_bias[None], rope_tables(length))
    marks = [3 * wide, 3 * wide + units, 3 * wide + 2 * units]

    def pieces(packed):
        return jnp.split(packed, marks, 1)

    weights = (qkv_weight, up_weight, down_weight, out_weight)

    def near_sums(outs):
        held = {k: [outs[k], [swap(x, "mp", mp, 1) for x in outs[k | 1]]] for k in reversed(range(0, mp, 2))}
        return held, far_gives(held, mp_bits[1:2])

    def far_gives(held, bits):
        gone = [k for k in held if k & bits[0]] if bits else []
        return {k: [sum(x[w].astype(F32) for x in held[k]).astype(BF) for w in range(2)] for k in gone}

    def far_sums(held, gives, which, wait):
        terms = {k: [x[which] for x in held[k]] for k in held}
        moved = None
        for i, bit in enumerate(mp_bits[1:]):
            for k in [k for k in terms if k & bit]:
                gone = terms.pop(k)
                give = sum(x.astype(F32) for x in gone).astype(BF) if i else gives[k][which]
                moved = swap(after(give, *wait), "mp", mp, bit)
                terms[k ^ bit].append(moved)
        return terms[0], moved

    def woven(one, two):
        return [x for pair in zip(one, two) for x in pair]

    prepared = prepare_call(me[None], weights, f_split, sources, sizes, dp)
    prepared = [prepared[0], prepared[1], prepared[2]]
    acc = None
    partials, totals = [], []
    far = far_rows(0, (both,))
    for c in range(chunks):
        begin, seqs = plan[c]
        scal = jnp.concatenate([lengths[begin : begin + seqs], me[None]])
        wait = (prepared[2],) if c == 0 else (partials[-1][0][0],)
        received = near_rows(far, wait)
        if c + 1 < chunks:
            far = far_rows(c + 1, (received[-1],))
        if c:
            held, gives = near_sums(partials[-1])
            ended = [far_sums(held, gives, w, (received[-1],)) for w in range(2)]
            moved = [x[1] for x in ended if x[1] is not None]
            totals.append(woven(ended[0][0], ended[1][0]))
            scal = after(scal, *[x for give in gives.values() for x in give])
        found = block_call(
            begin, seqs, c == chunks - 1, sizes, acc, scal, whole_rows, received, small, prepared,
            length, mp,
        )
        partials.append([found[2 * k : 2 * k + 2] for k in range(mp)])
        acc = after(found[2 * mp :], *moved) if c else found[2 * mp :]

    split_sum, *input_sums = acc
    grads_both = reduce_inputs(input_sums, sizes, dim, dp, mp)
    held, gives = near_sums(partials[-1])
    split_sum = after(split_sum, *[x for give in gives.values() for x in give])
    last_result, _ = far_sums(held, gives, 0, (grads_both,))
    owned = reduce_rows(jnp.concatenate([grads_both.astype(BF), split_sum], 1), dp)
    own_both, split_grad = owned[:, : grads_both.shape[1]], owned[:, grads_both.shape[1] :]
    cut = own_both.shape[1] - 2 * own_cols
    in_grad = own_both[:, :cut].reshape(own_ranks, 2, -1, rank).transpose(1, 2, 0, 3).reshape(in_factor.shape)
    res_grad = jnp.stack([own_both[:, cut : cut + own_cols], own_both[:, cut + own_cols :]])
    qkv_owned, up_owned, down_owned, out_owned = pieces(split_grad)
    down_owned, out_owned = down_owned.T, out_owned.T
    new_in, in_pruned = adam_step(in_factor, in_moments, in_grad)
    new_qkv, qkv_pruned = adam_step(qkv_factor, qkv_moments, qkv_owned)
    new_up, up_pruned = adam_step(up_factor, up_moments, up_owned)
    new_out, out_pruned = adam_step(out_factor, out_moments, out_owned)
    new_down, down_pruned = adam_step(down_factor, down_moments, down_owned)
    new_res, res_pruned = adam_step(res_factor, res_moments, res_grad)
    both = spread_inputs(low(new_in), low(new_res), mp, last_result[-1:])
    last_grad, _ = far_sums(held, gives, 1, (both,))
    totals.append(woven(last_result, last_grad))
    merged_qkv, merged_up, merged_down, merged_out = merge_call(
        me[None], weights,
        *gather_factors(both, rank_rows(new_qkv, new_up, new_down, new_out), sizes, dim, dp, mp), sizes, dp,
    )
    ended = []
    for c in range(chunks):
        ended = finish_call(
            plan[c][0], lengths[plan[c][0] : sum(plan[c])], totals[c], tokens, cotangent, res_bias, length, ended
        )
    result, grad_tokens = ended
    return (
        result,
        grad_tokens,
        in_grad,
        qkv_owned,
        up_owned,
        out_owned,
        down_owned,
        res_grad,
        merged_qkv,
        merged_out,
        merged_up,
        merged_down,
        in_pruned,
        qkv_pruned,
        up_pruned,
        out_pruned,
        down_pruned,
        res_pruned,
    )


def solution(mesh):
    placed = (
        P("dp", "mp"),
        P("dp", "mp"),
        P("dp"),
        P(),
        P(),
        P(None, "mp"),
        P("mp", None),
        P(None, "mp"),
        P("mp", None),
        P("mp"),
        P("mp"),
        P(None, "mp"),
        P(None, ("dp", "mp"), None),
        P("dp", "mp"),
        P("dp", "mp"),
        P("mp", "dp"),
        P("mp", "dp"),
        P(None, "dp", "mp"),
        P(None, None, ("dp", "mp"), None),
        P(None, "dp", "mp"),
        P(None, "dp", "mp"),
        P(None, "mp", "dp"),
        P(None, "mp", "dp"),
        P(None, None, "dp", "mp"),
    )
    return jax.shard_map(
        functools.partial(per_device, mesh.shape["dp"], mesh.shape["mp"]),
        mesh=mesh,
        in_specs=placed,
        out_specs=(
            P("dp", "mp"),
            P("dp", "mp"),
            P(None, ("dp", "mp"), None),
            P("dp", "mp"),
            P("dp", "mp"),
            P("mp", "dp"),
            P("mp", "dp"),
            P(None, "dp", "mp"),
            P(None, "mp"),
            P("mp", None),
            P(None, "mp"),
            P("mp", None),
            P(None, None, ("dp", "mp"), None),
            P(None, "dp", "mp"),
            P(None, "dp", "mp"),
            P(None, "mp", "dp"),
            P(None, "mp", "dp"),
            P(None, None, "dp", "mp"),
        ),
        check_vma=False,
    )
```

```python
import functools
import math

import jax
import jax.numpy as jnp
import numpy as np
from jax import lax
from jax.experimental import pallas as pl
from jax.experimental.pallas import tpu as pltpu
from jax.sharding import PartitionSpec as P

HEAD = 64
ROT = 16
BF = jnp.bfloat16
F32 = jnp.float32

first_fix = 1.0 - math.exp(100.0 * math.log(0.9))
second_fix = 1.0 - math.exp(100.0 * math.log(0.999))


def mm(a, b):
    return lax.dot_general(a, b, (((1,), (0,)), ((), ())), preferred_element_type=F32)


def mm_t(a, b):
    return lax.dot_general(a, b, (((1,), (1,)), ((), ())), preferred_element_type=F32)


def rows_mm(a, b):
    return lax.dot_general(a, b, (((0,), (0,)), ((), ())), preferred_element_type=F32)


def layer_norm(x):
    centred = x - jnp.mean(x, -1, keepdims=True)
    scale = lax.rsqrt(jnp.mean(centred * centred, -1, keepdims=True) + 1e-05)
    return centred * scale, scale


def layer_norm_back(grad_unit, unit_rows, scale):
    return scale * (
        grad_unit
        - jnp.mean(grad_unit, -1, keepdims=True)
        - unit_rows * jnp.mean(grad_unit * unit_rows, -1, keepdims=True)
    )


def rotate(values, cos, sin_a, sin_b, sign):
    width = values.shape[-1]
    turned = pltpu.roll(values, width - ROT // 2, 1) * sin_a + pltpu.roll(values, ROT // 2, 1) * sin_b
    return values * cos + turned if sign > 0 else values * cos - turned


def input_pairs(sizes, core, sources, fin_v, res_places):
    high, folds, ranks, rank, own_cols, direct = sizes
    if not direct:
        f_in, f_res = sources
        return [(f_in, fin_v), (f_res.at[0], res_places[0]), (f_res.at[1], res_places[1])]
    width = 2 * folds * rank + 2 * own_cols
    found = []
    for c in range(2):
        deep, wide2 = sources[c], sources[2 + c]
        which = core if c == 0 else 1 - core
        for y in range(high):
            for n in range(2):
                for j in range(folds):
                    at = y * width + (n * folds + j) * rank
                    rows = pl.ds(pl.multiple_of(((y * 2 + which) * folds + j) * ranks, ranks), ranks)
                    found.append((deep.at[:, :, at : at + rank], fin_v.at[n, :, rows, :]))
                at = y * width + 2 * folds * rank + n * own_cols
                place = pl.ds(pl.multiple_of((y * 2 + which) * own_cols, own_cols), own_cols)
                found.append((wide2.at[:, at : at + own_cols], res_places[n].at[:, place]))
    return found


def block_kernel(cfg, scal, *refs):
    chunk, seqs, first, last, length, tile, parts, cols, dim, wide, units, rank, sizes = cfg
    whole_rows, refs = refs[:4], refs[4:]
    received, refs = refs[: 2 * parts - 4], refs[2 * parts - 4 :]
    (gain, shift, b_qkv, b_up, rope, w_qkv, w_up, w_down), refs = refs[:8], refs[8:]
    (acc_in, res_in), refs = refs[:2], refs[2:]
    outs, refs = refs[: 2 * parts], refs[2 * parts :]
    sums, refs = refs[: len(refs) - 29], refs[len(refs) - 29 :]
    (
        gin_b, gres_b, gsplit_b, x_v, c_v, wq_v, wu_v, wd_v, rope_v, acc_v, res_v,
        q_s, k_s, v_s, g_s, qt_s, gt_s, gq_s, gkt_s, gvt_s, ac_s, p_s, qr_s, gor_s, out_v,
        row_sems, w_sems, out_sems, acc_sems,
    ) = refs
    me = scal[seqs]
    core = lax.rem(me, 2)
    steps = length // tile
    mixed_cols = 3 * wide
    joint = units + wide

    def tiles_of(s):
        return (scal[s] + tile - 1) // tile

    def row_slice(t, size=tile):
        return pl.ds(pl.multiple_of(t * tile, tile), size)


    def row_copies(s, t):
        found = []
        slot = lax.rem(s, 2)
        for which, dest in enumerate((x_v, c_v)):
            for k in range(parts):
                at = pl.ds(pl.multiple_of(s * length + t * tile, tile), tile)
                if k < 2:
                    src = whole_rows[2 * k + which].at[
                        pl.ds(pl.multiple_of((chunk + s) * length + t * tile, tile), tile), :
                    ]
                else:
                    src = received[2 * (k - 2) + which].at[at, :]
                place = pl.ds(pl.multiple_of(jnp.bitwise_xor(me, k) * cols, cols), cols)
                found.append(
                    pltpu.make_async_copy(
                        src, dest.at[slot, row_slice(t), place], row_sems.at[slot, t, which * parts + k]
                    )
                )
        return found

    def start_rows(s):
        def one(t, carry):
            for copy in row_copies(s, t):
                copy.start()
            return carry

        lax.fori_loop(0, tiles_of(s), one, 0)

    def out_copies(s, t):
        found = []
        for which in range(2):
            for k in range(parts):
                place = pl.ds(pl.multiple_of(jnp.bitwise_xor(me, k) * cols, cols), cols)
                rows = pl.ds(pl.multiple_of(s * length + t * tile, tile), tile)
                found.append(
                    pltpu.make_async_copy(
                        out_v.at[which, row_slice(t), place],
                        outs[2 * k + which].at[rows, :],
                        out_sems.at[t, which * parts + k],
                    )
                )
        return found

    def drain(s):
        def one(t, carry):
            for copy in out_copies(s, t):
                copy.wait()
            return carry

        lax.fori_loop(0, tiles_of(s), one, 0)

    pairs = [(w_up, wu_v), (w_down, wd_v), (w_qkv, wq_v), (rope, rope_v)]
    loads = [pltpu.make_async_copy(a, b, w_sems.at[i]) for i, (a, b) in enumerate(pairs)]
    start_rows(0)
    for load in loads:
        load.start()
    back_in = []
    if first:
        acc_v[...] = jnp.zeros_like(acc_v)
        res_v[...] = jnp.zeros_like(res_v)
    else:
        back_in = [
            pltpu.make_async_copy(acc_in, acc_v, acc_sems.at[0]),
            pltpu.make_async_copy(res_in, res_v, acc_sems.at[1]),
        ]
        for copy in back_in:
            copy.start()
    for load in loads:
        load.wait()
    for copy in back_in:
        copy.wait()
    c_in0, c_in1, c_qkv, c_up, c_down, c_out = (
        slice(0, dim),
        slice(dim, 2 * dim),
        slice(2 * dim, 2 * dim + mixed_cols),
        slice(2 * dim + mixed_cols, 2 * dim + mixed_cols + units),
        slice(2 * dim + mixed_cols + units, 2 * dim + mixed_cols + 2 * units),
        slice(2 * dim + mixed_cols + 2 * units, 2 * dim + mixed_cols + 2 * units + wide),
    )
    lane = lax.broadcasted_iota(jnp.int32, (1, 128), 1)
    left = lane < HEAD

    def one_sequence(s, carry):
        seq_len = scal[s]
        count = tiles_of(s)
        slot = lax.rem(s, 2)

        @pl.when(s + 1 < seqs)
        def _():
            start_rows(s + 1)

        gkt_s[...] = jnp.zeros_like(gkt_s)
        gvt_s[...] = jnp.zeros_like(gvt_s)

        def upstream(t, size):
            position = t * tile + lax.broadcasted_iota(jnp.int32, (size, 1), 0)
            return jnp.where(position < seq_len, c_v[slot, row_slice(t, size), :].astype(F32), 0.0).astype(BF)

        def tables(t, size):
            rows = row_slice(t, size)
            return [jnp.concatenate([rope_v[i, rows, :]] * (wide // 128), 1) for i in range(3)]

        def forward(t, size):
            rows = row_slice(t, size)
            for j in range(size // tile):
                for copy in row_copies(s, t + j):
                    copy.wait()
            unit, _ = layer_norm(x_v[slot, rows, :].astype(F32))
            low_one = (unit * gain[0:1, :] + shift[0:1, :]).astype(BF)
            low_two = (unit * gain[1:2, :] + shift[1:2, :]).astype(BF)
            ups = upstream(t, size)
            hidden = mm(low_two, wu_v[:dim, :])
            back = mm_t(ups, wd_v[:, :dim])
            mixed = mm(low_one, wq_v[:dim, :])
            code_up = hidden[:, units:]
            hidden = hidden[:, :units] + b_up[...]
            code_qkv = mixed[:, mixed_cols:]
            mixed = mixed[:, :mixed_cols] + mm(code_qkv.astype(BF), wq_v[dim:, :mixed_cols]) + b_qkv[...]
            blocks = [mixed[:, i * 128 : (i + 1) * 128] for i in range(mixed_cols // 128)]
            cat = lambda found: jnp.concatenate(found, 1) if len(found) > 1 else found[0]
            q_mixed = cat([jnp.where(left, blocks[3 * p], blocks[3 * p + 1]) for p in range(wide // 128)])
            k_mixed = cat(
                [pltpu.roll(jnp.where(left, blocks[3 * p + 2], blocks[3 * p]), HEAD, 1) for p in range(wide // 128)]
            )
            v_mixed = cat([jnp.where(left, blocks[3 * p + 1], blocks[3 * p + 2]) for p in range(wide // 128)])
            cdf = 0.5 * (1.0 + lax.erf(hidden * (1.0 / math.sqrt(2.0))))
            active = (hidden * cdf).astype(BF)
            slope = cdf + hidden * (jnp.exp(-0.5 * hidden * hidden) * (1.0 / math.sqrt(2.0 * math.pi)))
            grad_hidden = (back[:, :units] * slope).astype(BF)
            ac_s[rows, :units] = active
            cos, sin_a, sin_b = tables(t, size)
            query = rotate(q_mixed, cos, sin_a, sin_b, 1).astype(BF).astype(F32) * HEAD**-0.5
            q_s[rows, :] = query.astype(BF)
            qt_s[:, rows] = query.T.astype(BF)
            k_s[rows, :] = rotate(k_mixed, cos, sin_a, sin_b, 1).astype(BF)
            v_s[rows, :] = v_mixed.astype(BF)
            qr_s[:, rows] = code_qkv.T.astype(BF)
            grad_context = back[:, units:joint]
            g_s[rows, :] = grad_context.astype(BF)
            gt_s[:, rows] = grad_context.T.astype(BF)
            gor_s[:, rows] = back[:, joint + rank :].T.astype(BF)
            below = mm_t(grad_hidden, wu_v[:, :units])
            p_s[rows, :] = below[:, :dim] * gain[1:2, :]
            acc_v[:, c_up] += mm(code_up.T.astype(BF), grad_hidden)
            acc_v[:, c_down] += mm(back[:, joint : joint + rank].T.astype(BF), active)
            acc_v[:, c_in1] += mm(below[:, dim:].T.astype(BF), low_two)

        def finish(t, size):
            rows = row_slice(t, size)
            cos, sin_a, sin_b = tables(t, size)
            grad_q = rotate(gq_s[rows, :], cos, sin_a, sin_b, -1)
            grad_k = rotate(gkt_s[:, rows].T, cos, sin_a, sin_b, -1)
            grad_v = gvt_s[:, rows].T
            blocks = []
            for p in range(wide // 128):
                pair = slice(p * 128, (p + 1) * 128)
                one_q, one_k, one_v = grad_q[:, pair], pltpu.roll(grad_k[:, pair], HEAD, 1), grad_v[:, pair]
                blocks += [jnp.where(left, one_q, one_k), jnp.where(left, one_v, one_q), jnp.where(left, one_k, one_v)]
            grad_mixed = jnp.concatenate(blocks, 1).astype(BF)
            below = mm_t(grad_mixed, wq_v[:, :mixed_cols])
            both = ac_s[rows, :]
            ahead = mm(both, wd_v[:joint, :])
            unit, scale = layer_norm(x_v[slot, rows, :].astype(F32))
            low_one = (unit * gain[0:1, :] + shift[0:1, :]).astype(BF)
            out_v[0, rows, :] = ahead[:, :dim].astype(BF)
            grad_code = below[:, dim:]
            grad_norm = below[:, :dim] + mm_t(grad_code.astype(BF), wq_v[:dim, mixed_cols:])
            grad_unit = grad_norm * gain[0:1, :] + p_s[rows, :]
            out_v[1, rows, :] = layer_norm_back(grad_unit, unit, scale).astype(BF)
            for j in range(size // tile):
                for copy in out_copies(s, t + j):
                    copy.start()
            acc_v[:, c_in0] += mm(grad_code.T.astype(BF), low_one)
            acc_v[:, c_qkv] += mm(qr_s[:, rows], grad_mixed)
            acc_v[:, c_out] += mm(gor_s[:, rows], both[:, units:])
            res_v[...] += mm(ahead[:, dim:].T.astype(BF), upstream(t, size))

        def over_rows(work):
            def single(j, carry):
                work(j, tile)
                return carry

            lax.fori_loop(0, count, single, 0)

        over_rows(forward)

        for i in range(steps):
            @pl.when(i < count)
            def _(i=i):
                qrows = pl.ds(i * tile, tile)
                before, extent = i * tile, (i + 1) * tile
                qpos = before + lax.broadcasted_iota(jnp.int32, (tile, tile), 0)
                kpos = before + lax.broadcasted_iota(jnp.int32, (tile, tile), 1)
                allowed = (kpos <= qpos) & (kpos < seq_len)
                allowed = jnp.concatenate([allowed, allowed], 0)
                def one_pair(p, carry):
                    pair = pl.ds(pl.multiple_of(p * 128, 128), 128)
                    q_all, g_all = q_s[qrows, pair], g_s[qrows, pair]
                    zero = jnp.zeros_like(q_all)
                    q_two = jnp.concatenate([jnp.where(left, q_all, zero), jnp.where(left, zero, q_all)], 0)
                    g_two = jnp.concatenate([jnp.where(left, g_all, zero), jnp.where(left, zero, g_all)], 0)
                    keys, vals = k_s[:extent, pair], v_s[:extent, pair]
                    scores = mm_t(q_two, keys)
                    grad_probs = mm_t(g_two, vals)
                    last = jnp.where(allowed, scores[:, before:], -1e30)
                    scores = jnp.concatenate([scores[:, :before], last], 1) if i else last
                    weights = jnp.exp(scores - jnp.max(scores, -1, keepdims=True))
                    probs = weights * (1.0 / jnp.sum(weights, -1, keepdims=True))
                    low_probs = probs.astype(BF)
                    context = mm(low_probs, vals)
                    row_term = jnp.sum(probs * grad_probs, -1, keepdims=True)
                    grad_scores = (probs * (grad_probs - row_term)).astype(BF)
                    grad_q = mm(grad_scores, keys)
                    ac_s[qrows, pl.ds(pl.multiple_of(units + p * 128, 128), 128)] = jnp.where(
                        left, context[:tile], context[tile:]
                    ).astype(BF)
                    gq_s[qrows, pair] = jnp.where(left, grad_q[:tile], grad_q[tile:]) * HEAD**-0.5
                    for h in range(2):
                        feats = pl.ds(pl.multiple_of(p * 128 + h * HEAD, HEAD), HEAD)
                        part = slice(h * tile, (h + 1) * tile)
                        gkt_s[feats, :extent] += mm(qt_s[feats, qrows], grad_scores[part])
                        gvt_s[feats, :extent] += mm(gt_s[feats, qrows], low_probs[part])
                    return carry

                lax.fori_loop(0, wide // 128, one_pair, 0)

        @pl.when(s > 0)
        def _():
            drain(s - 1)

        over_rows(finish)
        return carry

    lax.fori_loop(0, seqs, one_sequence, 0)
    if not last:
        targets = [(acc_v, sums[0]), (res_v, sums[1])]
    else:
        high, folds, ranks, _, own_cols, direct = sizes
        gsplit_b[...] = acc_v[:, 2 * dim :].astype(BF)
        gres_b[:rank, :] = res_v[rank:, :].astype(BF)
        gres_b[rank:, :] = res_v[:rank, :].astype(BF)
        for n, place in enumerate((c_in0, c_in1)):
            gin_b[n] = acc_v[:, place].T.astype(BF).reshape(gin_b.shape[1:])
        targets = [(gsplit_b, sums[0])]
        if not direct:
            targets += [(gin_b, sums[1]), (gres_b, sums[2])]
        else:
            for c in range(2):
                which = core if c == 0 else 1 - core
                for y in range(high):
                    for n in range(2):
                        for j in range(folds):
                            at = (n * folds + j) * rank
                            rows = pl.ds(pl.multiple_of(((y * 2 + which) * folds + j) * ranks, ranks), ranks)
                            targets.append((gin_b.at[n, :, rows, :], sums[1 + c].at[y, :, :, at : at + rank]))
                        place = pl.ds(pl.multiple_of((y * 2 + which) * own_cols, own_cols), own_cols)
                        targets.append(
                            (gres_b.at[n * rank : (n + 1) * rank, place],
                             sums[3 + c].at[y, :, n * own_cols : (n + 1) * own_cols])
                        )
    back_out = [pltpu.make_async_copy(a, b, acc_sems.at[2 + i]) for i, (a, b) in enumerate(targets)]
    for copy in back_out:
        copy.start()
    drain(seqs - 1)
    for copy in back_out:
        copy.wait()


def prepare_kernel(cfg, scal, *refs):
    sizes, dim, wide, units, rank, n_src = cfg
    (w_qkv, w_up, w_down, w_out, f_split), refs = refs[:5], refs[5:]
    sources, refs = refs[:n_src], refs[n_src:]
    outs, (wq_v, wu_v, wd_v, ft_v, fin_v, w_sems, out_sems) = refs[:3], refs[3:]
    core = lax.rem(scal[0], 2)
    mixed_cols = 3 * wide
    joint = units + wide
    skip = f_split.shape[1] - mixed_cols - units - joint
    res_places = (wd_v.at[joint + rank :, :dim], wd_v.at[joint : joint + rank, :dim])
    pairs = [
        (w_qkv, wq_v.at[:dim, :mixed_cols]),
        (f_split.at[:, skip : skip + mixed_cols], wq_v.at[dim:, :mixed_cols]),
        (w_up, wu_v.at[:dim, :units]),
        (f_split.at[:, skip + mixed_cols : skip + mixed_cols + units], wu_v.at[dim:, :units]),
        (w_down, wd_v.at[:units, :dim]),
        (w_out, wd_v.at[units:joint, :dim]),
        (f_split.at[:, skip + mixed_cols + units :], ft_v),
    ] + input_pairs(sizes, core, sources, fin_v, res_places)
    loads = [pltpu.make_async_copy(a, b, w_sems.at[i]) for i, (a, b) in enumerate(pairs)]
    for load in loads:
        load.start()
    wd_v[:units, dim + rank :] = jnp.zeros((units, rank), BF)
    wd_v[units:joint, dim : dim + rank] = jnp.zeros((wide, rank), BF)
    wq_v[dim:, mixed_cols:] = jnp.zeros((rank, rank), BF)
    wu_v[dim:, units:] = jnp.zeros((rank, rank), BF)
    wd_v[joint:, dim:] = jnp.zeros((2 * rank, 2 * rank), BF)
    for load in loads:
        load.wait()
    wd_v[:units, dim : dim + rank] = ft_v[:, :units].astype(F32).T.astype(BF)
    wd_v[units:joint, dim + rank :] = ft_v[:, units:].astype(F32).T.astype(BF)
    wq_v[:dim, mixed_cols:] = fin_v[0].reshape(dim, rank)
    wu_v[:dim, units:] = fin_v[1].reshape(dim, rank)

    def whole(ref, top, depth, width, cut, other, at):
        def one(i, carry):
            rows = pl.ds(pl.multiple_of(top + i * cut, cut), cut)
            low_rank = mm(ref[rows, at : at + rank], other())
            ref[rows, :width] = (ref[rows, :width].astype(F32) + low_rank).astype(BF)
            return carry

        lax.fori_loop(0, depth // cut, one, 0)

    cut = min(256, units, wide)
    whole(wu_v, 0, dim, units, cut, lambda: wu_v[dim:, :units], units)
    whole(wd_v, 0, units, dim, cut, lambda: wd_v[joint : joint + rank, :dim], dim)
    whole(wd_v, units, wide, dim, cut, lambda: wd_v[joint + rank :, :dim], dim + rank)
    stores = [pltpu.make_async_copy(a, b, out_sems.at[i]) for i, (a, b) in enumerate(zip((wq_v, wu_v, wd_v), outs))]
    for store in stores:
        store.start()
    for store in stores:
        store.wait()


def prepare_call(scal, weights, f_split, sources, sizes, dp):
    w_qkv, w_up, w_down, w_out = weights
    dim, units, wide, rank = w_up.shape[0], w_up.shape[1], w_out.shape[0], f_split.shape[0]
    high, folds, ranks, _, own_cols, direct = sizes
    ANY = pl.BlockSpec(memory_space=pl.ANY)
    shapes = [(dim + rank, 3 * wide + rank), (dim + rank, units + rank), (units + wide + 2 * rank, dim + 2 * rank)]
    return pl.pallas_call(
        functools.partial(prepare_kernel, (sizes, dim, wide, units, rank, len(sources))),
        out_shape=[jax.ShapeDtypeStruct(shape, BF) for shape in shapes],
        in_specs=[pl.BlockSpec(memory_space=pltpu.SMEM)] + [ANY] * (5 + len(sources)),
        out_specs=[ANY] * 3,
        scratch_shapes=[pltpu.VMEM(shape, BF) for shape in shapes]
        + [
            pltpu.VMEM((rank, units + wide), BF),
            pltpu.VMEM((2, dp, dim // dp, rank), BF),
            pltpu.SemaphoreType.DMA((7 + (4 * high * (folds + 1) if direct else 3),)),
            pltpu.SemaphoreType.DMA((3,)),
        ],
        compiler_params=pltpu.CompilerParams(vmem_limit_bytes=60 * 1024 * 1024),
        cost_estimate=pl.CostEstimate(
            flops=2 * rank * dim * (2 * units + wide), bytes_accessed=16 * 1024 * 1024, transcendentals=0
        ),
        name="prepare",
    )(scal, *weights, f_split, *sources)


def block_call(chunk, seqs, last, sizes, acc, scal, whole_rows, received, small, weights, length, parts):
    gain, shift, b_qkv, b_up, rope = small
    high, folds, ranks, rank, own_cols, direct = sizes
    dim, units = weights[1].shape[0] - rank, weights[1].shape[1] - rank
    wide = weights[2].shape[0] - 2 * rank - units
    dp = rank // ranks
    cols = dim // parts
    tile = 256 if length % 256 == 0 else 128
    steps = length // tile
    first = acc is None
    acc_shape = jax.ShapeDtypeStruct((rank, 2 * dim + 4 * wide + 2 * units), F32)
    res_shape = jax.ShapeDtypeStruct((2 * rank, dim), F32)
    if first:
        acc = (jnp.zeros((8, 128), F32), jnp.zeros((8, 128), F32))
    cfg = (chunk, seqs, first, last, length, tile, parts, cols, dim, wide, units, rank, sizes)
    ANY = pl.BlockSpec(memory_space=pl.ANY)
    VM = pl.BlockSpec(memory_space=pltpu.VMEM)
    operands = [scal, *whole_rows, *received, gain, shift, b_qkv, b_up, rope, *weights, *acc]
    specs = [pl.BlockSpec(memory_space=pltpu.SMEM)] + [ANY] * (2 * parts) + [VM] * 4 + [ANY] * 6
    flops = 2 * seqs * length * (dim * (units * 4 + wide * 8 + rank * 12) + units * rank * 6 + length * wide * 12)
    out = [jax.ShapeDtypeStruct((seqs * length, cols), BF)] * (2 * parts)
    if not last:
        sums = [acc_shape, res_shape]
    else:
        sums = [jax.ShapeDtypeStruct((rank, 4 * wide + 2 * units), BF)]
        if direct:
            sums += [jax.ShapeDtypeStruct((high, dp, ranks, 2 * folds * rank), BF)] * 2
            sums += [jax.ShapeDtypeStruct((high, rank, 2 * own_cols), BF)] * 2
        else:
            sums += [jax.ShapeDtypeStruct((2, dp, dim // dp, rank), BF), jax.ShapeDtypeStruct((2 * rank, dim), BF)]
    in_shape = (2, dp, dim // dp, rank)
    tall = lambda n, dtype: pltpu.VMEM((length, n), dtype)
    flat = lambda n, dtype: pltpu.VMEM((n, length), dtype)
    return pl.pallas_call(
        functools.partial(block_kernel, cfg),
        out_shape=[*out, *sums],
        in_specs=specs,
        out_specs=[ANY] * (2 * parts + len(sums)),
        scratch_shapes=[
            pltpu.VMEM(in_shape if last else (2, 1, 16, rank), BF),
            pltpu.VMEM((2 * rank, dim) if last else (16, 128), BF),
            pltpu.VMEM((rank, 4 * wide + 2 * units) if last else (16, 128), BF),
            pltpu.VMEM((2, length, dim), BF),
            pltpu.VMEM((2, length, dim), BF),
            pltpu.VMEM((dim + rank, 3 * wide + rank), BF),
            pltpu.VMEM((dim + rank, units + rank), BF),
            pltpu.VMEM((units + wide + 2 * rank, dim + 2 * rank), BF),
            pltpu.VMEM(rope.shape, F32),
            pltpu.VMEM(acc_shape.shape, F32),
            pltpu.VMEM(res_shape.shape, F32),
            tall(wide, BF), tall(wide, BF), tall(wide, BF), tall(wide, BF),
            flat(wide, BF), flat(wide, BF),
            tall(wide, F32), flat(wide, F32), flat(wide, F32),
            tall(units + wide, BF), tall(dim, F32),
            flat(rank, BF), flat(rank, BF),
            pltpu.VMEM((2, length, dim), BF),
            pltpu.SemaphoreType.DMA((2, steps, 2 * parts)),
            pltpu.SemaphoreType.DMA((4,)),
            pltpu.SemaphoreType.DMA((steps, 2 * parts)),
            pltpu.SemaphoreType.DMA((5 + 4 * high * (folds + 1),)),
        ],
        input_output_aliases={} if first or last else {len(operands) - 2: 2 * parts, len(operands) - 1: 2 * parts + 1},
        compiler_params=pltpu.CompilerParams(vmem_limit_bytes=60 * 1024 * 1024),
        cost_estimate=pl.CostEstimate(
            flops=2 * flops, bytes_accessed=32 * 1024 * 1024, transcendentals=2 * seqs * length * units
        ),
        name="block",
    )(*operands)


def finish_kernel(cfg, lens, *refs):
    terms, block, length, aliased = cfg
    parts, refs = refs[:terms], refs[terms:]
    tokens, cotangent, bias = refs[:3]
    result, grad = refs[-2:]
    at = pl.program_id(0) * block
    seq_len = lens[at // length]
    position = at % length + lax.broadcasted_iota(jnp.int32, (block, 1), 0)
    valid = position < seq_len
    total = [sum(part[...].astype(F32) for part in parts[w::2]) for w in range(2)]
    result[...] = jnp.where(valid, tokens[...].astype(F32) + total[0] + bias[0:1, :] + bias[1:2, :], 0.0)
    grad[...] = jnp.where(valid, cotangent[...].astype(F32) + total[1], 0.0)


def finish_call(chunk, lens, parts, tokens, cotangent, bias, length, earlier):
    rows, cols = tokens.shape
    span = parts[0].shape[0]
    block = min(512, length)
    base = chunk * length // block
    part_spec = pl.BlockSpec((block, cols), lambda i: (i, 0))
    row_spec = pl.BlockSpec((block, cols), lambda i: (base + i, 0))
    specs = [pl.BlockSpec(memory_space=pltpu.SMEM)] + [part_spec] * len(parts) + [row_spec] * 2
    specs += [pl.BlockSpec(bias.shape, lambda i: (0, 0))] + [pl.BlockSpec(memory_space=pl.ANY)] * len(earlier)
    operands = [lens, *parts, tokens, cotangent, bias, *earlier]
    return pl.pallas_call(
        functools.partial(finish_kernel, (len(parts), block, length, bool(earlier))),
        grid=(span // block,),
        out_shape=[jax.ShapeDtypeStruct((rows, cols), F32)] * 2,
        in_specs=specs,
        out_specs=[row_spec] * 2,
        input_output_aliases={len(operands) - 2: 0, len(operands) - 1: 1} if earlier else {},
        cost_estimate=pl.CostEstimate(flops=8 * span * cols, bytes_accessed=20 * span * cols, transcendentals=0),
        name="finish",
    )(*operands)


def merge_kernel(cfg, scal, *refs):
    sizes, dim, wide, units, rank, n_src, cut = cfg
    (w_qkv, w_up, w_down, w_out, f_split), refs = refs[:5], refs[5:]
    sources, refs = refs[:n_src], refs[n_src:]
    outs, refs = refs[:4], refs[4:]
    weights_v, outs_v, (fin_v, res0_v, res1_v, split_v, t_v, in_sems, out_sems) = refs[:4], refs[4:8], refs[8:]
    core = lax.rem(scal[0], 2)
    skip = f_split.shape[1] - split_v.shape[1]
    pairs = input_pairs(sizes, core, sources, fin_v, (res0_v, res1_v)) + [(f_split.at[:, skip:], split_v)]
    pairs += list(zip((w_qkv, w_up, w_down, w_out), weights_v))
    loads = [pltpu.make_async_copy(a, b, in_sems.at[i]) for i, (a, b) in enumerate(pairs)]
    for load in loads:
        load.start()
    for load in loads:
        load.wait()
    mixed = 3 * wide
    t_v[...] = split_v[:, mixed + units :].astype(F32).T.astype(BF)
    plans = [
        (0, dim, lambda rows: fin_v[0].reshape(dim, rank)[rows], lambda: split_v[:, :mixed]),
        (1, dim, lambda rows: fin_v[1].reshape(dim, rank)[rows], lambda: split_v[:, mixed : mixed + units]),
        (2, units, lambda rows: t_v[rows, :], lambda: res1_v[...]),
        (3, wide, lambda rows: t_v[units + rows.start : units + rows.stop, :], lambda: res0_v[...]),
    ]
    stores = []
    for which, depth, left, right in plans:
        for at in range(0, depth, cut):
            rows = slice(at, at + cut)
            outs_v[which][rows, :] = weights_v[which][rows, :].astype(F32) + mm(left(rows), right())
            copy = pltpu.make_async_copy(outs_v[which].at[rows, :], outs[which].at[rows, :], out_sems.at[len(stores)])
            copy.start()
            stores.append(copy)
    for copy in stores:
        copy.wait()


def merge_call(scal, weights, f_split, sources, sizes, dp):
    w_qkv, w_up, w_down, w_out = weights
    dim, units, wide, rank = w_up.shape[0], w_up.shape[1], w_out.shape[0], f_split.shape[0]
    high, folds, ranks, _, own_cols, direct = sizes
    cut = min(256, wide)
    ANY = pl.BlockSpec(memory_space=pl.ANY)
    chunks = (2 * dim + units + wide) // cut
    return pl.pallas_call(
        functools.partial(merge_kernel, (sizes, dim, wide, units, rank, len(sources), cut)),
        out_shape=[jax.ShapeDtypeStruct(w.shape, F32) for w in weights],
        in_specs=[pl.BlockSpec(memory_space=pltpu.SMEM)] + [ANY] * (5 + len(sources)),
        out_specs=[ANY] * 4,
        scratch_shapes=[pltpu.VMEM(w.shape, BF) for w in weights]
        + [pltpu.VMEM(w.shape, F32) for w in weights]
        + [
            pltpu.VMEM((2, dp, dim // dp, rank), BF),
            pltpu.VMEM((rank, dim), BF),
            pltpu.VMEM((rank, dim), BF),
            pltpu.VMEM((rank, 4 * wide + 2 * units), BF),
            pltpu.VMEM((units + wide, rank), BF),
            pltpu.SemaphoreType.DMA((5 + (4 * high * (folds + 1) if direct else 3),)),
            pltpu.SemaphoreType.DMA((chunks,)),
        ],
        compiler_params=pltpu.CompilerParams(vmem_limit_bytes=60 * 1024 * 1024),
        cost_estimate=pl.CostEstimate(
            flops=2 * rank * (dim * (3 * wide + 2 * units + wide)), bytes_accessed=20 * 1024 * 1024, transcendentals=0
        ),
        name="merge",
    )(scal, *weights, f_split, *sources)


def bits_of(size):
    return [1 << b for b in range(size.bit_length() - 1)]


def swap(x, axis, size, bit):
    return lax.ppermute(x, axis, [(i, i ^ bit) for i in range(size)])


def bit_value(axis, bit):
    return (lax.axis_index(axis) // bit) % 2


def halve(x, axis, size, bit):
    mine = bit_value(axis, bit)
    keep = lax.dynamic_index_in_dim(x, mine, 0, keepdims=False).astype(F32)
    give = lax.dynamic_index_in_dim(x, 1 - mine, 0, keepdims=False).astype(BF)
    return keep + swap(give, axis, size, bit).astype(F32)


def after(x, *earlier):
    return lax.optimization_barrier((x, earlier))[0]


def in_order(x, other, axis, bit):
    upper = bit_value(axis, bit) == 1
    return jnp.where(upper, other, x), jnp.where(upper, x, other)


def spread_inputs(low_in, low_res, mp, wait=()):
    own_rows, rank = low_in.shape[1:]
    own_ranks = low_res.shape[1]
    both = jnp.concatenate(
        [low_in[n, j * own_ranks : (j + 1) * own_ranks] for n in range(2) for j in range(own_rows // own_ranks)]
        + [low_res[0], low_res[1]],
        1,
    )
    if wait:
        both = after(both, *wait)
    for bit in bits_of(mp)[1:]:
        both = jnp.concatenate(in_order(both, swap(both, "mp", mp, bit), "mp", bit), 1)
    return both


def gather_rows(x, dp):
    found = lax.all_to_all(jnp.broadcast_to(x[None], (dp,) + x.shape), "dp", 0, 0, tiled=True)
    return found.reshape(dp * x.shape[0], x.shape[1])


def gather_factors(both, split, sizes, dim, dp, mp, wait=()):
    high, folds, ranks, rank, own_cols, direct = sizes
    found = gather_rows(jnp.concatenate([both, split], 1), dp)
    mine = found[:, : both.shape[1]]
    if wait:
        mine = after(mine, *wait)
    other = swap(mine, "mp", mp, 1)
    if direct:
        deep = lambda x: x.reshape(dp, ranks, x.shape[1])
        return found, [deep(found), deep(other), found, other]
    cores = jnp.stack(in_order(mine, other, "mp", 1)).reshape(2, dp, ranks, high, both.shape[1] // high)
    in_part = cores[..., : 2 * folds * rank].reshape(2, dp, ranks, high, 2, folds, rank)
    res_part = cores[..., 2 * folds * rank :].reshape(2, dp, ranks, high, 2, own_cols)
    whole_in = in_part.transpose(4, 1, 3, 0, 5, 2, 6).reshape(2, dp, dim // dp, rank)
    return found, [whole_in, res_part.transpose(4, 1, 2, 3, 0, 5).reshape(2, rank, dim)]


def reduce_inputs(sums, sizes, dim, dp, mp):
    high, folds, ranks, rank, own_cols, direct = sizes
    if direct:
        in_keep, in_send, res_keep, res_send = sums
        in_both = in_keep.astype(F32) + swap(in_send, "mp", mp, 1).astype(F32)
        res_both = res_keep.astype(F32) + swap(res_send, "mp", mp, 1).astype(F32)
        both = jnp.concatenate([in_both.reshape(high, rank, -1), res_both], 2)
    else:
        in_part = sums[0].reshape(2, dp, high, 2, folds, ranks, rank)
        in_part = in_part.transpose(3, 2, 1, 5, 0, 4, 6).reshape(2, high, rank, 2 * folds * rank)
        res_part = sums[1].reshape(2, rank, high, 2, own_cols).transpose(3, 2, 1, 0, 4)
        both = halve(jnp.concatenate([in_part, res_part.reshape(2, high, rank, 2 * own_cols)], 3), "mp", mp, 1)
    both = both.reshape((2,) * len(bits_of(high)) + both.shape[1:])
    for bit in reversed(bits_of(mp)[1:]):
        both = halve(both, "mp", mp, bit)
    return both


def reduce_rows(x, dp):
    return jnp.sum(lax.all_to_all(x.reshape(dp, -1, x.shape[1]), "dp", 0, 0, tiled=True).astype(F32), 0)


def adam_step(factor, moment, gradient):
    first_moment = 0.9 * moment[0] + 0.1 * gradient
    second_moment = 0.999 * moment[1] + 0.001 * gradient * gradient
    updated = factor - 0.01 * (first_moment / first_fix) / (
        jnp.sqrt(second_moment / second_fix) + 1e-08
    )
    keep_mask = (jnp.abs(moment[0]) >= 0.5).astype(F32)
    return (updated, jnp.stack([first_moment * keep_mask, second_moment * keep_mask]))


def rope_tables(length):
    half = ROT // 2
    frequency = 10000.0 ** (-np.arange(half) * 2.0 / ROT)
    angles = np.arange(length)[:, None] * frequency[None, :]
    cos, sin = np.cos(angles), np.sin(angles)
    ones, zeros = np.ones((length, HEAD - ROT)), np.zeros((length, HEAD - ROT))
    blank = np.zeros_like(sin)
    one_head = [
        np.concatenate([cos, cos, ones], 1),
        np.concatenate([-sin, blank, zeros], 1),
        np.concatenate([blank, sin, zeros], 1),
    ]
    return jnp.asarray(np.stack([np.concatenate([t, t], 1) for t in one_head]).astype(np.float32))


def per_device(
    dp,
    mp,
    tokens,
    cotangent,
    lengths,
    norm_gain,
    norm_shift,
    qkv_weight,
    out_weight,
    up_weight,
    down_weight,
    qkv_bias,
    up_bias,
    res_bias,
    in_factor,
    qkv_factor,
    up_factor,
    out_factor,
    down_factor,
    res_factor,
    in_moments,
    qkv_moments,
    up_moments,
    out_moments,
    down_moments,
    res_moments,
):
    row_count, cols = tokens.shape
    seq_count = lengths.shape[0]
    length = row_count // seq_count
    wide = out_weight.shape[0]
    dim, units = up_weight.shape
    me = lax.axis_index("mp").astype(jnp.int32)
    mp_bits = bits_of(mp)
    plan = [(0, 2), (2, seq_count - 2)]
    chunks = len(plan)

    rank = in_factor.shape[2]
    low = lambda f: f.astype(BF)
    both = spread_inputs(low(in_factor), low(res_factor), mp)

    own_ranks, own_cols = res_factor.shape[1:]
    sizes = (mp // 2, in_factor.shape[1] // own_ranks, own_ranks, rank, own_cols, own_ranks % 16 == 0)
    rank_rows = lambda qkv, up, down, out: jnp.concatenate([low(qkv), low(up), low(down).T, low(out).T], 1)
    first_rows = [after(x[: plan[0][1] * length], both) for x in (tokens, cotangent)]
    f_split, sources = gather_factors(
        after(both, *first_rows), rank_rows(qkv_factor, up_factor, down_factor, out_factor), sizes, dim, dp, mp
    )
    whole_rows = (tokens, cotangent, swap(tokens, "mp", mp, 1), swap(cotangent, "mp", mp, 1))

    def far_rows(c, wait):
        rows = slice(plan[c][0] * length, sum(plan[c]) * length)
        held = {0: first_rows if c == 0 else [tokens[rows], cotangent[rows]]}
        for bit in reversed(mp_bits[1:]):
            for k in list(held):
                held[k | bit] = [swap(after(x, *wait), "mp", mp, bit) for x in held[k]]
        return {k: v for k, v in held.items() if k}

    def near_rows(held, wait):
        for k in list(held):
            held[k | 1] = [swap(after(x, *wait) if wait else x, "mp", mp, 1) for x in held[k]]
        return [x for k in sorted(held) for x in held[k]]

    small = (norm_gain, norm_shift, qkv_bias[None], up_bias[None], rope_tables(length))
    marks = [3 * wide, 3 * wide + units, 3 * wide + 2 * units]

    def pieces(packed):
        return jnp.split(packed, marks, 1)

    weights = (qkv_weight, up_weight, down_weight, out_weight)

    def near_sums(outs):
        held = {k: [outs[k], [swap(x, "mp", mp, 1) for x in outs[k | 1]]] for k in reversed(range(0, mp, 2))}
        return held, far_gives(held, mp_bits[1:2])

    def far_gives(held, bits):
        gone = [k for k in held if k & bits[0]] if bits else []
        return {k: [sum(x[w].astype(F32) for x in held[k]).astype(BF) for w in range(2)] for k in gone}

    def far_sums(held, gives, which, wait):
        terms = {k: [x[which] for x in held[k]] for k in held}
        moved = None
        for i, bit in enumerate(mp_bits[1:]):
            for k in [k for k in terms if k & bit]:
                gone = terms.pop(k)
                give = sum(x.astype(F32) for x in gone).astype(BF) if i else gives[k][which]
                moved = swap(after(give, *wait), "mp", mp, bit)
                terms[k ^ bit].append(moved)
        return terms[0], moved

    def woven(one, two):
        return [x for pair in zip(one, two) for x in pair]

    prepared = prepare_call(me[None], weights, f_split, sources, sizes, dp)
    prepared = [prepared[0], prepared[1], prepared[2]]
    acc = None
    partials, totals = [], []
    far = far_rows(0, (both,))
    for c in range(chunks):
        begin, seqs = plan[c]
        scal = jnp.concatenate([lengths[begin : begin + seqs], me[None]])
        wait = (prepared[2],) if c == 0 else (partials[-1][0][0],)
        received = near_rows(far, wait)
        if c + 1 < chunks:
            far = far_rows(c + 1, (received[-1],))
        if c:
            held, gives = near_sums(partials[-1])
            ended = [far_sums(held, gives, w, (received[-1],)) for w in range(2)]
            moved = [x[1] for x in ended if x[1] is not None]
            totals.append(woven(ended[0][0], ended[1][0]))
            scal = after(scal, *[x for give in gives.values() for x in give])
        found = block_call(
            begin, seqs, c == chunks - 1, sizes, acc, scal, whole_rows, received, small, prepared,
            length, mp,
        )
        partials.append([found[2 * k : 2 * k + 2] for k in range(mp)])
        acc = after(found[2 * mp :], *moved) if c else found[2 * mp :]

    split_sum, *input_sums = acc
    grads_both = reduce_inputs(input_sums, sizes, dim, dp, mp)
    held, gives = near_sums(partials[-1])
    split_sum = after(split_sum, *[x for give in gives.values() for x in give])
    last_result, _ = far_sums(held, gives, 0, (grads_both,))
    owned = reduce_rows(jnp.concatenate([grads_both.astype(BF), split_sum], 1), dp)
    own_both, split_grad = owned[:, : grads_both.shape[1]], owned[:, grads_both.shape[1] :]
    cut = own_both.shape[1] - 2 * own_cols
    in_grad = own_both[:, :cut].reshape(own_ranks, 2, -1, rank).transpose(1, 2, 0, 3).reshape(in_factor.shape)
    res_grad = jnp.stack([own_both[:, cut : cut + own_cols], own_both[:, cut + own_cols :]])
    qkv_owned, up_owned, down_owned, out_owned = pieces(split_grad)
    down_owned, out_owned = down_owned.T, out_owned.T
    new_in, in_pruned = adam_step(in_factor, in_moments, in_grad)
    new_qkv, qkv_pruned = adam_step(qkv_factor, qkv_moments, qkv_owned)
    new_up, up_pruned = adam_step(up_factor, up_moments, up_owned)
    new_out, out_pruned = adam_step(out_factor, out_moments, out_owned)
    new_down, down_pruned = adam_step(down_factor, down_moments, down_owned)
    new_res, res_pruned = adam_step(res_factor, res_moments, res_grad)
    both = spread_inputs(low(new_in), low(new_res), mp, last_result[-1:])
    last_grad, _ = far_sums(held, gives, 1, (both,))
    totals.append(woven(last_result, last_grad))
    ended = []
    for c in range(chunks):
        ended = finish_call(
            plan[c][0], lengths[plan[c][0] : sum(plan[c])], totals[c], tokens, cotangent, res_bias, length, ended
        )
    moments = (in_pruned, qkv_pruned, up_pruned, out_pruned, down_pruned, res_pruned)
    merged_qkv, merged_up, merged_down, merged_out = merge_call(
        me[None], weights,
        *gather_factors(
            both, rank_rows(new_qkv, new_up, new_down, new_out), sizes, dim, dp, mp, (*ended, *moments)
        ),
        sizes, dp,
    )
    result, grad_tokens = ended
    return (
        result,
        grad_tokens,
        in_grad,
        qkv_owned,
        up_owned,
        out_owned,
        down_owned,
        res_grad,
        merged_qkv,
        merged_out,
        merged_up,
        merged_down,
        in_pruned,
        qkv_pruned,
        up_pruned,
        out_pruned,
        down_pruned,
        res_pruned,
    )


def solution(mesh):
    placed = (
        P("dp", "mp"),
        P("dp", "mp"),
        P("dp"),
        P(),
        P(),
        P(None, "mp"),
        P("mp", None),
        P(None, "mp"),
        P("mp", None),
        P("mp"),
        P("mp"),
        P(None, "mp"),
        P(None, ("dp", "mp"), None),
        P("dp", "mp"),
        P("dp", "mp"),
        P("mp", "dp"),
        P("mp", "dp"),
        P(None, "dp", "mp"),
        P(None, None, ("dp", "mp"), None),
        P(None, "dp", "mp"),
        P(None, "dp", "mp"),
        P(None, "mp", "dp"),
        P(None, "mp", "dp"),
        P(None, None, "dp", "mp"),
    )
    return jax.shard_map(
        functools.partial(per_device, mesh.shape["dp"], mesh.shape["mp"]),
        mesh=mesh,
        in_specs=placed,
        out_specs=(
            P("dp", "mp"),
            P("dp", "mp"),
            P(None, ("dp", "mp"), None),
            P("dp", "mp"),
            P("dp", "mp"),
            P("mp", "dp"),
            P("mp", "dp"),
            P(None, "dp", "mp"),
            P(None, "mp"),
            P("mp", None),
            P(None, "mp"),
            P("mp", None),
            P(None, None, ("dp", "mp"), None),
            P(None, "dp", "mp"),
            P(None, "dp", "mp"),
            P(None, "mp", "dp"),
            P(None, "mp", "dp"),
            P(None, None, "dp", "mp"),
        ),
        check_vma=False,
    )
```
